128 devices in a mesh: ctr: 16 (over y, x), bat: 8 (over z, core).
Axes of the slice: x: 4, y: 4, z: 4, core: 2. Of those that a mesh axis runs over, the one named last changes fastest.
Arguments:
- table: bfloat16 [131072, 1024], P('ctr'), may hold values from -6 to 6
- coefs: bfloat16 [131072, 256], P('ctr', 'bat'), may hold values from -6 to 6
- targets: float32 [1024, 256], P(None, 'bat'), may hold values from -6 to 6
- eigvecs: bfloat16 [65536, 256], P('ctr'), may hold values from -0.0234375 to 0.0234375
- correction: float32 [256], replicated, may hold values from 200 to 4000
- batch_idx: int32 [1024], P('bat'), may hold values from 0 to 131071
- nystrom_idx: int32 [65536], P('ctr'), may hold values from 0 to 131071, as said below
Outputs:
- residual: float32 [1024, 256], P(None, 'bat')
- nystrom_update: float32 [65536, 256], P('ctr', 'bat')
The draws below stay inside these ranges and needn't reach their ends.
Inputs may be any that keep to these rules, and one draw needn't show every extreme that they name: `nystrom_idx`: entry m names a row of the block of 8192 table rows numbered m // 4096.
All inputs are finite; a program needn't handle non-finite values.
Results may differ from the reference program's by a relative error of at most 0.0031.
Values may be sent and summed in bfloat16 or wider, within the bound.
No kernel may reach another device: no remote copies, remote signals or barrier semaphores. Data moves between devices by JAX's collectives and lax.ppermute only.
A program may use at most 128 MiB of HBM per device.

```python
import math
import jax
import jax.numpy as jnp
from jax import lax

D = 1024
O = 256
Q = 256
C_DEV = 8192
M_DEV = 4096
B = 1024
C = 131072
M = 65536
N_CTR = 16


def draw_nystrom_idx(key, part):
    key = jax.random.fold_in(key, 7)
    within = jax.random.randint(key, (M,), 0, C_DEV)
    owner = jnp.arange(M, dtype=jnp.int32) // M_DEV
    return (owner * C_DEV + within).astype(jnp.int32)


def place_ends(array, key, smallest, largest):
    place = [jax.random.randint(jax.random.fold_in(key, axis), (), 0, length) for axis, length in enumerate(array.shape)]
    widest = array.shape.index(max(array.shape))
    next_to = place[:widest] + [(place[widest] + 1) % array.shape[widest]] + place[widest + 1:]
    return array.at[tuple(place)].set(smallest).at[tuple(next_to)].set(largest)


def levels(stream_key, dims, pieces, least, high):
    def one(dim, parts):
        heights = jax.random.uniform(jax.random.fold_in(jax.random.fold_in(stream_key, 6), dim), (parts,), jnp.float32, least / len(pieces), high / len(pieces))
        return jnp.repeat(jnp.exp(heights), dims[dim] // parts).reshape((-1,) + (1,) * (len(dims) - dim - 1))

    factor_of = one(*pieces[0])
    for cut in pieces[1:]:
        factor_of = factor_of * one(*cut)
    return factor_of


def scatter_about(key, dims, deviation, limit, pieces=(), kind=jnp.bfloat16):
    factor_of = levels(key, dims, pieces, -0.22, 0.18) if pieces else 1.0
    array = jax.random.normal(key, dims, jnp.float32) * deviation * factor_of
    return jnp.minimum(jnp.maximum(array, -limit), limit).astype(kind)


def setup_inputs(seed: int = 0) -> dict:
    seeds = jax.random.split(jax.random.key(seed), 8)
    return {
        "table": scatter_about(seeds[0], (C, D), 1.0, 6.0, ((0, 16),)),
        "coefs": scatter_about(seeds[1], (C, O), 1.0, 6.0, ((0, 16), (1, 8))),
        "targets": scatter_about(seeds[2], (B, O), 1.0, 6.0, ((1, 8),), jnp.float32),
        "eigvecs": scatter_about(seeds[3], (M, Q), M ** -0.5, 0.0234375, ((0, 16),)),
        "correction": jnp.clip(jnp.exp(jax.random.uniform(seeds[4], (Q,), jnp.float32, math.log(200.0), math.log(4000.0))), 200.0, 4000.0),
        "batch_idx": place_ends(jax.random.randint(seeds[5], (B,), 0, C), jax.random.fold_in(seeds[5], 1), 0, C - 1).astype(jnp.int32),
        "nystrom_idx": draw_nystrom_idx(jax.random.fold_in(seeds[7], 71), 0),
    }


def kernel(left, right):
    sharpness = 4.0 / D
    left_sq = jnp.sum(left.astype(jnp.float32) ** 2, axis=1)
    right_sq = jnp.sum(right.astype(jnp.float32) ** 2, axis=1)
    cross = jnp.dot(left, right.T, preferred_element_type=jnp.float32)
    return jnp.exp(-sharpness * (left_sq[:, None] + right_sq[None, :] - 2.0 * cross))


def reference(table, coefs, targets, eigvecs, correction, batch_idx, nystrom_idx):
    points = jnp.take(table, batch_idx, axis=0)
    table_blocks = table.reshape(N_CTR, C_DEV, D)
    coef_blocks = coefs.reshape(N_CTR, C_DEV, O)

    def one_block(pair):
        kern = kernel(points, pair[0]).astype(jnp.bfloat16)
        return jnp.dot(kern, pair[1], preferred_element_type=jnp.float32)

    pred = jnp.sum(lax.map(one_block, (table_blocks, coef_blocks)), axis=0)
    residual = pred - targets
    grad = residual.astype(jnp.bfloat16)
    nystrom_rows = jnp.take(table, nystrom_idx, axis=0)
    kern_nys = kernel(nystrom_rows, points).astype(jnp.bfloat16)
    applied = jnp.dot(kern_nys, grad, preferred_element_type=jnp.float32)
    projected = jnp.dot(eigvecs.astype(jnp.float32).T, applied, precision=lax.Precision.HIGHEST)
    nystrom_update = jnp.dot(eigvecs.astype(jnp.float32), correction[:, None] * projected, precision=lax.Precision.HIGHEST)
    return residual, nystrom_update
```

```python
import functools

import jax
import jax.numpy as jnp
from jax import lax
from jax.experimental import pallas as pl
from jax.experimental.pallas import tpu as pltpu
from jax.sharding import PartitionSpec as P

D = 1024
SHARPNESS = 4.0 / D
N_CTR = 16
N_Z = 4
LANES = 128
GROUP = 16
MIB = 2**20
F32 = jnp.float32
BF16 = jnp.bfloat16
SMEM = pl.BlockSpec(memory_space=pltpu.SMEM)
VMEM = pl.BlockSpec(memory_space=pltpu.VMEM)
HBM = pl.BlockSpec(memory_space=pltpu.HBM)
SWAP = [(i, i ^ 1) for i in range(2 * N_Z)]
SAME_CORE = [[c * 8 + z * 2 + k for c in range(N_CTR) for z in range(N_Z)] for k in range(2)]


def z_shift(k):
    return [(z * 2 + c, (z + k) % N_Z * 2 + c) for z in range(N_Z) for c in range(2)]


def in_vmem(x):
    return pltpu.with_memory_space_constraint(x, pltpu.VMEM)


def pick_kernel(idx_ref, table_ref, out_ref, groups, rows, sems):
    n = rows.shape[0]
    c_rows = table_ref.shape[0]
    first_row = lax.axis_index("ctr") * c_rows
    rows[...] = jnp.zeros_like(rows)

    def copy_of(i, pos):
        start = pl.multiple_of(pos // GROUP * GROUP, GROUP)
        return pltpu.make_async_copy(table_ref.at[pl.ds(start, GROUP)], groups.at[i], sems.at[i])

    def start(i, carry):
        pos = idx_ref[i] - first_row

        @pl.when((pos >= 0) & (pos < c_rows))
        def _():
            copy_of(i, pos).start()

        return carry

    def finish(i, carry):
        pos = idx_ref[i] - first_row

        @pl.when((pos >= 0) & (pos < c_rows))
        def _():
            copy_of(i, pos).wait()
            group = groups[i].astype(F32)
            place = lax.broadcasted_iota(jnp.int32, group.shape, 0)
            kept = jnp.where(place == pos % GROUP, group, 0.0)
            rows[pl.ds(i, 1), :] = jnp.sum(kept, axis=0, keepdims=True)

        return carry

    lax.fori_loop(0, n, start, 0)
    lax.fori_loop(0, n, finish, 0)
    out_ref[...] = rows[...].astype(BF16)


def pick(batch_idx, table):
    n = batch_idx.shape[0]
    return pl.pallas_call(
        pick_kernel,
        in_specs=[SMEM, HBM],
        out_specs=VMEM,
        out_shape=jax.ShapeDtypeStruct((n, D), BF16),
        scratch_shapes=[
            pltpu.VMEM((n, GROUP, D), BF16),
            pltpu.VMEM((n, D), F32),
            pltpu.SemaphoreType.DMA((n,)),
        ],
        compiler_params=pltpu.CompilerParams(vmem_limit_bytes=8 * MIB),
        name="pick",
    )(batch_idx, pltpu.with_memory_space_constraint(table, pltpu.HBM))


def main_kernel(tile, idx_ref, pts_ref, table_ref, *rest):
    coef_refs = rest[:8]
    eig_ref, out_ref, kern, nys, acc = rest[8:]
    pts = pts_ref[...].astype(F32)
    pts_sq = lax.dot_general(
        jnp.ones((8, D), F32), pts * pts, (((1,), (1,)), ((), ())),
        precision=lax.Precision.HIGHEST, preferred_element_type=F32,
    )[0:1]
    acc[...] = jnp.zeros_like(acc)

    def one_tile(i, carry):
        rows = pl.ds(pl.multiple_of(i * tile, tile), tile)
        block = table_ref[rows, :]
        cross = lax.dot_general(
            block, pts_ref[...], (((1,), (1,)), ((), ())), preferred_element_type=F32
        )
        wide = block.astype(F32)
        row_sq = jnp.sum(wide * wide, axis=1, keepdims=True)
        k = jnp.exp(-SHARPNESS * (row_sq + pts_sq - 2.0 * cross)).astype(BF16)
        kern[rows, :] = k.astype(F32)
        coefs = jnp.concatenate([ref[:, rows] for ref in coef_refs], axis=0)
        acc[...] += jnp.dot(coefs, k, preferred_element_type=F32)
        return carry

    lax.fori_loop(0, table_ref.shape[0] // tile, one_tile, 0)

    unroll = 32

    def gather(j, carry):
        for u in range(unroll):
            m = j * unroll + u
            nys[pl.ds(m, 1), :] = kern[pl.ds(idx_ref[m], 1), :]
        return carry

    lax.fori_loop(0, nys.shape[0] // unroll, gather, 0)
    comp = lax.dot_general(
        eig_ref[...], nys[...].astype(BF16), (((0,), (0,)), ((), ())), preferred_element_type=F32
    )
    for c in range(N_CTR):
        out_ref[c, 0:16, :] = comp[c * 16:(c + 1) * 16]
    bat = lax.axis_index("bat")
    z = bat // 2
    core = bat % 2
    for k in range(N_Z):
        for s in range(2):
            from_z = (z + N_Z - k) % N_Z
            from_core = core if s == 0 else 1 - core
            piece = acc[(2 * k + s) * 32:(2 * k + s + 1) * 32, :]
            for i in range(8):
                out_ref[from_core * 8 + i, pl.ds(16 + from_z * 4, 4), :] = piece[4 * i:4 * i + 4]


def main(local_idx, points, table, pieces, eigvecs):
    c_rows = table.shape[0]
    m_rows, q = eigvecs.shape
    return pl.pallas_call(
        functools.partial(main_kernel, 1024),
        in_specs=[SMEM] + [VMEM] * 11,
        out_specs=VMEM,
        out_shape=jax.ShapeDtypeStruct((N_CTR, 32, LANES), F32),
        scratch_shapes=[
            pltpu.VMEM((c_rows, LANES), F32),
            pltpu.VMEM((m_rows, LANES), F32),
            pltpu.VMEM((q, LANES), F32),
        ],
        compiler_params=pltpu.CompilerParams(vmem_limit_bytes=20 * MIB),
        cost_estimate=pl.CostEstimate(flops=3 * 10**9, bytes_accessed=24 * MIB, transcendentals=10**6),
        name="main",
    )(local_idx, points, in_vmem(table), *[in_vmem(x) for x in pieces], in_vmem(eigvecs))


def split3(x):
    hi = x.astype(BF16)
    rest = x - hi.astype(F32)
    mid = rest.astype(BF16)
    lo = (rest - mid.astype(F32)).astype(BF16)
    return hi, mid, lo


def final_kernel(same_ref, other_ref, targets_ref, corr_ref, eig_ref, res_ref, upd_ref, comp):
    core = lax.axis_index("bat") % 2
    for z in range(N_Z):
        for s, ref in enumerate((same_ref, other_ref)):
            from_core = core if s == 0 else 1 - core
            lanes = pl.ds(pl.multiple_of((2 * z + from_core) * LANES, LANES), LANES)
            for c in range(N_CTR):
                comp[c * 16:(c + 1) * 16, lanes] = ref[c * N_Z + z, 0:16, :]
            for i in range(8):
                row = (core * 8 + i) * N_Z + z
                res_ref[4 * i:4 * i + 4, lanes] = ref[row, 16:20, :]
    residual = res_ref[...] - targets_ref[...]
    res_ref[...] = residual
    grad = residual.astype(BF16)
    proj = jnp.zeros((32, comp.shape[0]), F32)
    for part in split3(comp[...]):
        proj += lax.dot_general(grad, part, (((1,), (1,)), ((), ())), preferred_element_type=F32)
    scaled = jnp.concatenate(split3(proj * corr_ref[...]), axis=0)
    upd = lax.dot_general(
        scaled, eig_ref[...], (((1,), (1,)), ((), ())), preferred_element_type=F32
    )
    upd_ref[...] = upd[0:32] + (upd[32:64] + upd[64:96])


def final(same, other, targets, correction, eigvecs):
    cols, n = targets.shape
    m_rows, q = eigvecs.shape
    return pl.pallas_call(
        final_kernel,
        in_specs=[VMEM] * 5,
        out_specs=[VMEM, VMEM],
        out_shape=[
            jax.ShapeDtypeStruct((cols, n), F32),
            jax.ShapeDtypeStruct((cols, m_rows), F32),
        ],
        scratch_shapes=[pltpu.VMEM((q, n), F32)],
        compiler_params=pltpu.CompilerParams(vmem_limit_bytes=16 * MIB),
        name="final",
    )(same, other, targets, correction, in_vmem(eigvecs))


def per_device(table, coefs, targets, eigvecs, correction, batch_idx, nystrom_idx):
    c_rows = table.shape[0]
    first_row = lax.axis_index("ctr") * c_rows
    own = coefs.T
    from_z = [lax.ppermute(own, "bat", z_shift(k)) if k else own for k in range(N_Z)]

    picked = pick(batch_idx, table).reshape(N_CTR, -1, D)
    parts = lax.all_to_all(picked, "ctr", 0, 0)
    own_points = jnp.sum(parts.astype(F32), axis=0).astype(BF16)
    spread = jnp.broadcast_to(own_points[None], parts.shape)
    points = lax.all_to_all(spread, "ctr", 0, 0).reshape(-1, D)

    points, *from_z = lax.optimization_barrier((points, *from_z))
    pieces = [x for here in from_z for x in (here, lax.ppermute(here, "bat", SWAP))]
    partial = main(nystrom_idx - first_row, points, table, pieces, eigvecs)
    mine = jnp.sum(lax.all_to_all(partial, "ctr", 0, 0), axis=0)
    comp = jnp.broadcast_to(mine[None, :16], (N_Z, 16, LANES))
    pred = jnp.pad(mine[16:].reshape(N_Z, 4, LANES), ((0, 0), (0, 4), (0, 0)))
    sent = jnp.concatenate([comp, pred], axis=1)
    sent = jnp.broadcast_to(sent[None], (N_CTR,) + sent.shape).reshape((-1,) + sent.shape[1:])
    same = lax.all_to_all(sent, ("ctr", "bat"), 0, 0, axis_index_groups=SAME_CORE)
    other = lax.ppermute(same, "bat", SWAP)
    residual, update = final(same, other, targets.T, correction[None], eigvecs)
    return residual.T, update.T


def solution(mesh):
    return jax.shard_map(
        per_device,
        mesh=mesh,
        in_specs=(
            P("ctr", None),
            P("ctr", "bat"),
            P(None, "bat"),
            P("ctr", None),
            P(),
            P("bat"),
            P("ctr"),
        ),
        out_specs=(P(None, "bat"), P("ctr", "bat")),
        check_vma=False,
    )
```

```python
import functools

import jax
import jax.numpy as jnp
from jax import lax
from jax.experimental import pallas as pl
from jax.experimental.pallas import tpu as pltpu
from jax.sharding import PartitionSpec as P

D = 1024
SHARPNESS = 4.0 / D
N_CTR = 16
N_Z = 4
LANES = 128
GROUP = 16
MIB = 2**20
F32 = jnp.float32
BF16 = jnp.bfloat16
SMEM = pl.BlockSpec(memory_space=pltpu.SMEM)
VMEM = pl.BlockSpec(memory_space=pltpu.VMEM)
HBM = pl.BlockSpec(memory_space=pltpu.HBM)
SWAP = [(i, i ^ 1) for i in range(2 * N_Z)]
SAME_CORE = [[c * 8 + z * 2 + k for c in range(N_CTR) for z in range(N_Z)] for k in range(2)]


def z_shift(k):
    return [(z * 2 + c, (z + k) % N_Z * 2 + c) for z in range(N_Z) for c in range(2)]


def in_vmem(x):
    return pltpu.with_memory_space_constraint(x, pltpu.VMEM)


def pick_kernel(idx_ref, nys_ref, table_ref, out_ref, local_ref, listed, groups, rows, sems):
    n = rows.shape[0]
    c_rows = table_ref.shape[0]
    first_row = lax.axis_index("ctr") * c_rows

    def note(i, count):
        pos = idx_ref[i] - first_row
        listed[count] = i
        return count + jnp.where((pos >= 0) & (pos < c_rows), 1, 0)

    count = lax.fori_loop(0, n, note, 0, unroll=8)

    def copy_of(s):
        pos = idx_ref[listed[s]] - first_row
        start = pl.multiple_of(pos // GROUP * GROUP, GROUP)
        return pltpu.make_async_copy(table_ref.at[pl.ds(start, GROUP)], groups.at[s], sems.at[s])

    def start(s, carry):
        copy_of(s).start()
        return carry

    lax.fori_loop(0, count, start, 0)
    local_ref[...] = nys_ref[...] - first_row
    rows[...] = jnp.zeros_like(rows)

    def finish(s, carry):
        copy_of(s).wait()
        i = listed[s]
        group = groups[s].astype(F32)
        place = lax.broadcasted_iota(jnp.int32, group.shape, 0)
        kept = jnp.where(place == (idx_ref[i] - first_row) % GROUP, group, 0.0)
        rows[pl.ds(i, 1), :] = jnp.sum(kept, axis=0, keepdims=True)
        return carry

    lax.fori_loop(0, count, finish, 0)
    out_ref[...] = rows[...].astype(BF16)


def pick(batch_idx, nystrom_idx, table):
    n = batch_idx.shape[0]
    return pl.pallas_call(
        pick_kernel,
        in_specs=[SMEM, VMEM, HBM],
        out_specs=[VMEM, VMEM],
        out_shape=[
            jax.ShapeDtypeStruct((n, D), BF16),
            jax.ShapeDtypeStruct(nystrom_idx.shape, jnp.int32),
        ],
        scratch_shapes=[
            pltpu.SMEM((n + 1,), jnp.int32),
            pltpu.VMEM((n, GROUP, D), BF16),
            pltpu.VMEM((n, D), F32),
            pltpu.SemaphoreType.DMA((n,)),
        ],
        compiler_params=pltpu.CompilerParams(vmem_limit_bytes=8 * MIB),
        name="pick",
    )(batch_idx, nystrom_idx, pltpu.with_memory_space_constraint(table, pltpu.HBM))


N_TILES = 8


def main_kernel(idx_ref, pts_ref, table_ref, *rest):
    coef_refs = rest[:8]
    eig_ref, out_ref, held, cross, kern, kern16, nys, acc, sems = rest[8:]

    n_tiles = sems.shape[0]
    tile = held.shape[0] // n_tiles
    q = eig_ref.shape[1]

    def rows_of(i):
        return pl.ds(pl.multiple_of(i * tile, tile), tile)

    def copy_of(i):
        rows = rows_of(i)
        return pltpu.make_async_copy(table_ref.at[rows], held.at[rows], sems.at[i])

    for i in range(n_tiles):
        copy_of(i).start()
    pts = pts_ref[...].astype(F32)
    pts_sq = lax.dot_general(
        jnp.ones((8, D), F32), pts * pts, (((1,), (1,)), ((), ())),
        precision=lax.Precision.HIGHEST, preferred_element_type=F32,
    )[0:1]

    def multiply(i):
        copy_of(i).wait()
        cross[i % 2] = lax.dot_general(
            held[rows_of(i), :], pts_ref[...], (((1,), (1,)), ((), ())),
            preferred_element_type=F32,
        )

    def finish(i):
        wide = held[rows_of(i), :].astype(F32)
        row_sq = jnp.sum(wide * wide, axis=1, keepdims=True)
        k = jnp.exp(-SHARPNESS * (row_sq + pts_sq - 2.0 * cross[i % 2])).astype(BF16)
        kern[rows_of(i), :] = k.astype(F32)
        kern16[rows_of(i), :] = k

    def both(i, carry):
        multiply(i)
        finish(i - 1)
        return carry

    multiply(0)
    lax.fori_loop(1, n_tiles, both, 0)
    finish(n_tiles - 1)

    unroll = 32

    def gather(j, carry):
        for u in range(unroll):
            m = j * unroll + u
            nys[pl.ds(m, 1), :] = kern[pl.ds(idx_ref[m], 1), :]
        return carry

    lax.fori_loop(0, nys.shape[0] // unroll, gather, 0)
    coefs = jnp.concatenate([ref[...] for ref in coef_refs], axis=0)
    acc[...] = jnp.dot(coefs, kern16[...], preferred_element_type=F32)
    comp = lax.dot_general(
        eig_ref[...], nys[...].astype(BF16), (((0,), (0,)), ((), ())), preferred_element_type=F32
    )
    for c in range(N_CTR):
        out_ref[c, 0:16, :] = comp[c * 16:(c + 1) * 16]
    bat = lax.axis_index("bat")
    z = bat // 2
    core = bat % 2
    for k in range(N_Z):
        for s in range(2):
            from_z = (z + N_Z - k) % N_Z
            from_core = core if s == 0 else 1 - core
            first = (2 * k + s) * 32
            for i in range(8):
                out_ref[from_core * 8 + i, pl.ds(16 + from_z * 4, 4), :] = acc[first + 4 * i:first + 4 * i + 4]


def main(local_idx, points, table, pieces, eigvecs):
    c_rows = table.shape[0]
    m_rows, q = eigvecs.shape
    return pl.pallas_call(
        main_kernel,
        in_specs=[SMEM, VMEM, HBM] + [VMEM] * 9,
        out_specs=VMEM,
        out_shape=jax.ShapeDtypeStruct((N_CTR, 32, LANES), F32),
        scratch_shapes=[
            pltpu.VMEM((c_rows, D), BF16),
            pltpu.VMEM((2, c_rows // N_TILES, LANES), F32),
            pltpu.VMEM((c_rows, LANES), F32),
            pltpu.VMEM((c_rows, LANES), BF16),
            pltpu.VMEM((m_rows, LANES), F32),
            pltpu.VMEM((256, LANES), F32),
            pltpu.SemaphoreType.DMA((N_TILES,)),
        ],
        compiler_params=pltpu.CompilerParams(vmem_limit_bytes=40 * MIB),
        cost_estimate=pl.CostEstimate(flops=3 * 10**9, bytes_accessed=24 * MIB, transcendentals=10**6),
        name="main",
    )(
        local_idx, points, pltpu.with_memory_space_constraint(table, pltpu.HBM),
        *[in_vmem(x) for x in pieces], in_vmem(eigvecs),
    )


def split3(x):
    hi = x.astype(BF16)
    rest = x - hi.astype(F32)
    mid = rest.astype(BF16)
    lo = (rest - mid.astype(F32)).astype(BF16)
    return hi, mid, lo


def final_kernel(same_ref, other_ref, targets_ref, corr_ref, eig_ref, res_ref, upd_ref, comp):
    core = lax.axis_index("bat") % 2
    for z in range(N_Z):
        for s, ref in enumerate((same_ref, other_ref)):
            from_core = core if s == 0 else 1 - core
            lanes = pl.ds(pl.multiple_of((2 * z + from_core) * LANES, LANES), LANES)
            for c in range(N_CTR):
                comp[c * 16:(c + 1) * 16, lanes] = ref[c * N_Z + z, 0:16, :]
            for i in range(8):
                row = (core * 8 + i) * N_Z + z
                res_ref[4 * i:4 * i + 4, lanes] = ref[row, 16:20, :]
    residual = res_ref[...] - targets_ref[...]
    res_ref[...] = residual
    grad = residual.astype(BF16)
    proj = jnp.zeros((32, comp.shape[0]), F32)
    for part in split3(comp[...]):
        proj += lax.dot_general(grad, part, (((1,), (1,)), ((), ())), preferred_element_type=F32)
    scaled = jnp.concatenate(split3(proj * corr_ref[...]), axis=0)
    upd = lax.dot_general(
        scaled, eig_ref[...], (((1,), (1,)), ((), ())), preferred_element_type=F32
    )
    upd_ref[...] = upd[0:32] + (upd[32:64] + upd[64:96])


def final(same, other, targets, correction, eigvecs):
    cols, n = targets.shape
    m_rows, q = eigvecs.shape
    return pl.pallas_call(
        final_kernel,
        in_specs=[VMEM] * 5,
        out_specs=[VMEM, VMEM],
        out_shape=[
            jax.ShapeDtypeStruct((cols, n), F32),
            jax.ShapeDtypeStruct((cols, m_rows), F32),
        ],
        scratch_shapes=[pltpu.VMEM((q, n), F32)],
        compiler_params=pltpu.CompilerParams(vmem_limit_bytes=16 * MIB),
        name="final",
    )(same, other, targets, correction, in_vmem(eigvecs))


def per_device(table, coefs, targets, eigvecs, correction, batch_idx, nystrom_idx):
    picked, local_idx = pick(batch_idx, nystrom_idx.reshape(-1, LANES), table)
    picked, own = lax.optimization_barrier((picked.reshape(N_CTR, -1, D), coefs.T))
    from_z = [lax.ppermute(own, "bat", z_shift(k)) if k else own for k in range(N_Z)]

    parts = lax.all_to_all(picked, "ctr", 0, 0)
    own_points = jnp.sum(parts.astype(F32), axis=0).astype(BF16)
    spread = jnp.broadcast_to(own_points[None], parts.shape)
    points = lax.all_to_all(spread, "ctr", 0, 0).reshape(-1, D)

    points, *from_z = lax.optimization_barrier((points, *from_z))
    pieces = [x for here in from_z for x in (here, lax.ppermute(here, "bat", SWAP))]
    partial = main(local_idx.reshape(-1), points, table, pieces, eigvecs)
    mine = jnp.sum(lax.all_to_all(partial, "ctr", 0, 0), axis=0)
    comp = jnp.broadcast_to(mine[None, :16], (N_Z, 16, LANES))
    pred = jnp.pad(mine[16:].reshape(N_Z, 4, LANES), ((0, 0), (0, 4), (0, 0)))
    sent = jnp.concatenate([comp, pred], axis=1)
    sent = jnp.broadcast_to(sent[None], (N_CTR,) + sent.shape).reshape((-1,) + sent.shape[1:])
    same = lax.all_to_all(sent, ("ctr", "bat"), 0, 0, axis_index_groups=SAME_CORE)
    other = lax.ppermute(same, "bat", SWAP)
    residual, update = final(same, other, targets.T, correction[None], eigvecs)
    return residual.T, update.T


def solution(mesh):
    return jax.shard_map(
        per_device,
        mesh=mesh,
        in_specs=(
            P("ctr", None),
            P("ctr", "bat"),
            P(None, "bat"),
            P("ctr", None),
            P(),
            P("bat"),
            P("ctr"),
        ),
        out_specs=(P(None, "bat"), P("ctr", "bat")),
        check_vma=False,
    )
```

```python
import functools

import jax
import jax.numpy as jnp
from jax import lax
from jax.experimental import pallas as pl
from jax.experimental.pallas import tpu as pltpu
from jax.sharding import PartitionSpec as P

D = 1024
SHARPNESS = 4.0 / D
N_CTR = 16
N_Z = 4
LANES = 128
GROUP = 16
SLOTS = 24
MIB = 2**20
F32 = jnp.float32
BF16 = jnp.bfloat16
SMEM = pl.BlockSpec(memory_space=pltpu.SMEM)
VMEM = pl.BlockSpec(memory_space=pltpu.VMEM)
HBM = pl.BlockSpec(memory_space=pltpu.HBM)
SWAP = [(i, i ^ 1) for i in range(2 * N_Z)]
SAME_CORE = [[c * 8 + z * 2 + k for c in range(N_CTR) for z in range(N_Z)] for k in range(2)]


def z_shift(k):
    return [(z * 2 + c, (z + k) % N_Z * 2 + c) for z in range(N_Z) for c in range(2)]


def in_vmem(x):
    return pltpu.with_memory_space_constraint(x, pltpu.VMEM)


def pick_kernel(first, *refs):
    round_ref = None if first else refs[0]
    idx_hbm, table_ref, out_ref, rounds_ref, idx_ref, counts, listed, groups, rows, sems = refs[0 if first else 1:]
    n = listed.shape[0] - 1
    c_rows = table_ref.shape[0]
    ctr = lax.axis_index("ctr")
    idx_copy = pltpu.make_async_copy(idx_hbm, idx_ref, sems.at[SLOTS])
    idx_copy.start()
    rows[...] = jnp.zeros_like(rows)
    for c in range(N_CTR):
        counts[c] = 0
    idx_copy.wait()

    def note(i, most):
        owner = idx_ref[i] // c_rows
        count = counts[owner]
        listed[jnp.where(owner == ctr, count, n)] = i
        counts[owner] = count + 1
        return jnp.maximum(most, count + 1)

    most = lax.fori_loop(0, n, note, 0, unroll=8)
    rounds_ref[0] = (most + SLOTS - 1) // SLOTS
    done = 0 if first else round_ref[0] * SLOTS
    count = jnp.clip(counts[ctr] - done, 0, SLOTS)

    def copy_of(s):
        pos = idx_ref[listed[done + s]] - ctr * c_rows
        start = pl.multiple_of(pos // GROUP * GROUP, GROUP)
        return pltpu.make_async_copy(table_ref.at[pl.ds(start, GROUP)], groups.at[s], sems.at[s])

    def start(s, carry):
        copy_of(s).start()
        return carry

    def finish(s, carry):
        copy_of(s).wait()
        group = groups[s].astype(F32)
        place = lax.broadcasted_iota(jnp.int32, group.shape, 0)
        kept = jnp.where(place == idx_ref[listed[done + s]] % GROUP, group, 0.0)
        rows[pl.ds(s, 1), :] = jnp.sum(kept, axis=0, keepdims=True)
        return carry

    lax.fori_loop(0, count, start, 0)
    lax.fori_loop(0, count, finish, 0)
    packed = rows[...].astype(BF16)
    for c in range(N_CTR):
        out_ref[c] = packed


def pick(batch_idx, table, at_round=None):
    n = batch_idx.shape[0]
    first = at_round is None
    return pl.pallas_call(
        functools.partial(pick_kernel, first),
        in_specs=([] if first else [SMEM]) + [HBM, HBM],
        out_specs=[VMEM, SMEM],
        out_shape=[
            jax.ShapeDtypeStruct((N_CTR, SLOTS, D), BF16),
            jax.ShapeDtypeStruct((1,), jnp.int32),
        ],
        scratch_shapes=[
            pltpu.SMEM((n,), jnp.int32),
            pltpu.SMEM((N_CTR,), jnp.int32),
            pltpu.SMEM((n + 1,), jnp.int32),
            pltpu.VMEM((SLOTS, GROUP, D), BF16),
            pltpu.VMEM((SLOTS, D), F32),
            pltpu.SemaphoreType.DMA((SLOTS + 1,)),
        ],
        compiler_params=pltpu.CompilerParams(vmem_limit_bytes=8 * MIB),
        name="pick",
    )(
        *([] if first else [at_round]),
        pltpu.with_memory_space_constraint(batch_idx, pltpu.HBM),
        pltpu.with_memory_space_constraint(table, pltpu.HBM),
    )


def settled(idx_row, received, at_round, c_rows):
    n = idx_row.shape[1]
    owner_row = (idx_row // c_rows).astype(F32)
    i = lax.broadcasted_iota(jnp.int32, (n, n), 0)
    j = lax.broadcasted_iota(jnp.int32, (n, n), 1)
    owner = jnp.sum(jnp.where(i == j, owner_row, 0.0), axis=1, keepdims=True)
    before = (owner == owner_row) & (j < i)
    slot = jnp.sum(jnp.where(before, 1.0, 0.0), axis=1, keepdims=True) - at_round * SLOTS
    here = (slot >= 0.0) & (slot < SLOTS)
    place = jnp.where(here, owner * SLOTS + slot, -1.0)
    column = lax.broadcasted_iota(jnp.int32, (n, N_CTR * SLOTS), 1).astype(F32)
    chosen = jnp.where(column == place, 1.0, 0.0).astype(BF16)
    return jnp.dot(chosen, received, preferred_element_type=F32)


def settle_kernel(c_rows, round_ref, idx_ref, received_ref, before_ref, out_ref):
    at_round = round_ref[0].astype(F32)
    rows = settled(idx_ref[...], received_ref[...], at_round, c_rows)
    out_ref[...] = (rows + before_ref[...].astype(F32)).astype(BF16)


def settle(at_round, idx_row, received, before, c_rows):
    return pl.pallas_call(
        functools.partial(settle_kernel, c_rows),
        in_specs=[SMEM, VMEM, VMEM, VMEM],
        out_specs=VMEM,
        out_shape=jax.ShapeDtypeStruct(before.shape, BF16),
        compiler_params=pltpu.CompilerParams(vmem_limit_bytes=8 * MIB),
        name="settle",
    )(at_round, idx_row, received, before)


N_TILES = 8


def kern_kernel(
    idx_ref, received_ref, more_ref, nys_ref, table_ref, kern, kern16, local_ref, held, pts_ref, cross, sems
):
    n_tiles = sems.shape[0]
    c_rows = held.shape[0]
    tile = c_rows // n_tiles

    def rows_of(i):
        return pl.ds(pl.multiple_of(i * tile, tile), tile)

    def copy_of(i):
        rows = rows_of(i)
        return pltpu.make_async_copy(table_ref.at[rows], held.at[rows], sems.at[i])

    for i in range(n_tiles):
        copy_of(i).start()
    local_ref[...] = nys_ref[...] - lax.axis_index("ctr") * c_rows
    pts = settled(idx_ref[...], received_ref[...], 0.0, c_rows) + more_ref[...].astype(F32)
    pts_ref[...] = pts.astype(BF16)
    pts_sq = lax.dot_general(
        jnp.ones((8, D), F32), pts * pts, (((1,), (1,)), ((), ())),
        precision=lax.Precision.HIGHEST, preferred_element_type=F32,
    )[0:1]

    def multiply(i):
        copy_of(i).wait()
        cross[i % 2] = lax.dot_general(
            held[rows_of(i), :], pts_ref[...], (((1,), (1,)), ((), ())),
            preferred_element_type=F32,
        )

    def finish(i):
        wide = held[rows_of(i), :].astype(F32)
        row_sq = jnp.sum(wide * wide, axis=1, keepdims=True)
        k = jnp.exp(-SHARPNESS * (row_sq + pts_sq - 2.0 * cross[i % 2])).astype(BF16)
        kern[rows_of(i), :] = k.astype(F32)
        kern16[rows_of(i), :] = k

    def both(i, carry):
        multiply(i)
        finish(i - 1)
        return carry

    multiply(0)
    lax.fori_loop(1, n_tiles, both, 0)
    finish(n_tiles - 1)


def kernel_rows(idx_row, received, more, nystrom_idx, table):
    c_rows = table.shape[0]
    n = idx_row.shape[1]
    return pl.pallas_call(
        kern_kernel,
        in_specs=[VMEM, VMEM, VMEM, VMEM, HBM],
        out_specs=[VMEM, VMEM, VMEM],
        out_shape=[
            jax.ShapeDtypeStruct((c_rows, n), F32),
            jax.ShapeDtypeStruct((c_rows, n), BF16),
            jax.ShapeDtypeStruct(nystrom_idx.shape, jnp.int32),
        ],
        scratch_shapes=[
            pltpu.VMEM((c_rows, D), BF16),
            pltpu.VMEM((n, D), BF16),
            pltpu.VMEM((2, c_rows // N_TILES, n), F32),
            pltpu.SemaphoreType.DMA((N_TILES,)),
        ],
        compiler_params=pltpu.CompilerParams(vmem_limit_bytes=30 * MIB),
        cost_estimate=pl.CostEstimate(flops=10**10, bytes_accessed=24 * MIB, transcendentals=10**6),
        name="kernel_rows",
    )(idx_row, received, more, nystrom_idx, pltpu.with_memory_space_constraint(table, pltpu.HBM))


def comp_kernel(idx_ref, kern, eig_ref, out_ref, nys):
    unroll = 32

    def gather(j, carry):
        for u in range(unroll):
            m = j * unroll + u
            nys[pl.ds(m, 1), :] = kern[pl.ds(idx_ref[m], 1), :]
        return carry

    lax.fori_loop(0, nys.shape[0] // unroll, gather, 0)
    out_ref[...] = lax.dot_general(
        eig_ref[...], nys[...].astype(BF16), (((0,), (0,)), ((), ())), preferred_element_type=F32
    )


def components(local_idx, kern, eigvecs):
    m_rows, q = eigvecs.shape
    n = kern.shape[1]
    return pl.pallas_call(
        comp_kernel,
        in_specs=[SMEM, VMEM, VMEM],
        out_specs=VMEM,
        out_shape=jax.ShapeDtypeStruct((q, n), F32),
        scratch_shapes=[pltpu.VMEM((m_rows, n), F32)],
        compiler_params=pltpu.CompilerParams(vmem_limit_bytes=16 * MIB),
        cost_estimate=pl.CostEstimate(flops=5 * 10**9, bytes_accessed=6 * MIB, transcendentals=0),
        name="components",
    )(local_idx, kern, in_vmem(eigvecs))


def pred_kernel(comp_ref, kern16, *rest):
    coef_refs = rest[:8]
    out_ref, acc = rest[8:]
    coefs = jnp.concatenate([ref[...] for ref in coef_refs], axis=0)
    acc[...] = jnp.dot(coefs, kern16[...], preferred_element_type=F32)
    for c in range(N_CTR):
        out_ref[c, 0:16, :] = comp_ref[c * 16:(c + 1) * 16, :]
    bat = lax.axis_index("bat")
    z = bat // 2
    core = bat % 2
    for k in range(N_Z):
        for s in range(2):
            from_z = (z + N_Z - k) % N_Z
            from_core = core if s == 0 else 1 - core
            first = (2 * k + s) * 32
            for i in range(8):
                out_ref[from_core * 8 + i, pl.ds(16 + from_z * 4, 4), :] = acc[first + 4 * i:first + 4 * i + 4]


def predict(comp, kern16, pieces):
    return pl.pallas_call(
        pred_kernel,
        in_specs=[VMEM] * 10,
        out_specs=VMEM,
        out_shape=jax.ShapeDtypeStruct((N_CTR, 32, LANES), F32),
        scratch_shapes=[pltpu.VMEM((256, LANES), F32)],
        compiler_params=pltpu.CompilerParams(vmem_limit_bytes=16 * MIB),
        name="predict",
    )(comp, kern16, *[in_vmem(x) for x in pieces])


def split3(x):
    hi = x.astype(BF16)
    rest = x - hi.astype(F32)
    mid = rest.astype(BF16)
    lo = (rest - mid.astype(F32)).astype(BF16)
    return hi, mid, lo


def final_kernel(same_ref, other_ref, targets_ref, corr_ref, eig_ref, res_ref, upd_ref, comp):
    core = lax.axis_index("bat") % 2
    for z in range(N_Z):
        for s, ref in enumerate((same_ref, other_ref)):
            from_core = core if s == 0 else 1 - core
            lanes = pl.ds(pl.multiple_of((2 * z + from_core) * LANES, LANES), LANES)
            for c in range(N_CTR):
                comp[c * 16:(c + 1) * 16, lanes] = ref[c * N_Z + z, 0:16, :]
            for i in range(8):
                row = (core * 8 + i) * N_Z + z
                res_ref[4 * i:4 * i + 4, lanes] = ref[row, 16:20, :]
    residual = res_ref[...] - targets_ref[...]
    res_ref[...] = residual
    grad = residual.astype(BF16)
    proj = jnp.zeros((32, comp.shape[0]), F32)
    for part in split3(comp[...]):
        proj += lax.dot_general(grad, part, (((1,), (1,)), ((), ())), preferred_element_type=F32)
    scaled = jnp.concatenate(split3(proj * corr_ref[...]), axis=0)
    upd = lax.dot_general(
        scaled, eig_ref[...], (((1,), (1,)), ((), ())), preferred_element_type=F32
    )
    upd_ref[...] = upd[0:32] + (upd[32:64] + upd[64:96])


def final(same, other, targets, correction, eigvecs):
    cols, n = targets.shape
    m_rows, q = eigvecs.shape
    return pl.pallas_call(
        final_kernel,
        in_specs=[VMEM] * 5,
        out_specs=[VMEM, VMEM],
        out_shape=[
            jax.ShapeDtypeStruct((cols, n), F32),
            jax.ShapeDtypeStruct((cols, m_rows), F32),
        ],
        scratch_shapes=[pltpu.VMEM((q, n), F32)],
        compiler_params=pltpu.CompilerParams(vmem_limit_bytes=16 * MIB),
        name="final",
    )(same, other, targets, correction, in_vmem(eigvecs))


def per_device(table, coefs, targets, eigvecs, correction, batch_idx, nystrom_idx):
    c_rows = table.shape[0]
    picked, rounds = pick(batch_idx, table)
    picked, own = lax.optimization_barrier((picked, coefs.T))
    from_z = [lax.ppermute(own, "bat", z_shift(k)) if k else own for k in range(N_Z)]

    idx_row = batch_idx.reshape(1, -1)
    received = lax.all_to_all(picked, "ctr", 0, 0).reshape(-1, D)

    def further(state):
        at_round, more = state
        sent, _ = pick(batch_idx, table, at_round.reshape(1))
        got = lax.all_to_all(sent, "ctr", 0, 0).reshape(-1, D)
        return at_round + 1, settle(at_round.reshape(1), idx_row, got, more, c_rows)

    none = jnp.zeros((batch_idx.shape[0], D), BF16)
    _, more = lax.while_loop(lambda state: state[0] < rounds[0], further, (jnp.int32(1), none))

    kern, kern16, local_idx = kernel_rows(
        idx_row, received, more, nystrom_idx.reshape(-1, LANES), table
    )
    kern, *from_z = lax.optimization_barrier((kern, *from_z))
    pieces = [x for here in from_z for x in (here, lax.ppermute(here, "bat", SWAP))]
    comp = components(local_idx.reshape(-1), kern, eigvecs)
    comp, *pieces = lax.optimization_barrier((comp, *pieces))
    partial = predict(comp, kern16, pieces)
    mine = jnp.sum(lax.all_to_all(partial, "ctr", 0, 0), axis=0)
    comp = jnp.broadcast_to(mine[None, :16], (N_Z, 16, LANES))
    pred = jnp.pad(mine[16:].reshape(N_Z, 4, LANES), ((0, 0), (0, 4), (0, 0)))
    sent = jnp.concatenate([comp, pred], axis=1)
    sent = jnp.broadcast_to(sent[None], (N_CTR,) + sent.shape).reshape((-1,) + sent.shape[1:])
    same = lax.all_to_all(sent, ("ctr", "bat"), 0, 0, axis_index_groups=SAME_CORE)
    other = lax.ppermute(same, "bat", SWAP)
    residual, update = final(same, other, targets.T, correction[None], eigvecs)
    return residual.T, update.T


def solution(mesh):
    return jax.shard_map(
        per_device,
        mesh=mesh,
        in_specs=(
            P("ctr", None),
            P("ctr", "bat"),
            P(None, "bat"),
            P("ctr", None),
            P(),
            P("bat"),
            P("ctr"),
        ),
        out_specs=(P(None, "bat"), P("ctr", "bat")),
        check_vma=False,
    )
```

```python
import functools

import jax
import jax.numpy as jnp
from jax import lax
from jax.experimental import pallas as pl
from jax.experimental.pallas import tpu as pltpu
from jax.sharding import PartitionSpec as P

D = 1024
SHARPNESS = 4.0 / D
N_CTR = 16
N_Z = 4
LANES = 128
GROUP = 16
SLOTS = 24
PARTS = ((0, 2048), (2048, 2048))
MIB = 2**20
F32 = jnp.float32
BF16 = jnp.bfloat16
SMEM = pl.BlockSpec(memory_space=pltpu.SMEM)
VMEM = pl.BlockSpec(memory_space=pltpu.VMEM)
HBM = pl.BlockSpec(memory_space=pltpu.HBM)
ANY = pl.BlockSpec(memory_space=pl.ANY)
SWAP = [(i, i ^ 1) for i in range(2 * N_Z)]
SAME_CORE = [[c * 8 + z * 2 + k for c in range(N_CTR) for z in range(N_Z)] for k in range(2)]


def z_shift(k):
    return [(z * 2 + c, (z + k) % N_Z * 2 + c) for z in range(N_Z) for c in range(2)]


def in_vmem(x):
    return pltpu.with_memory_space_constraint(x, pltpu.VMEM)


def in_hbm(x):
    return pltpu.with_memory_space_constraint(x, pltpu.HBM)


def pick_kernel(first, *refs):
    round_ref = None if first else refs[0]
    idx_hbm, table_ref, out_ref, rounds_ref, idx_ref, counts, listed, groups, rows, sems = refs[0 if first else 1:]
    n = listed.shape[0] - 1
    c_rows = table_ref.shape[0]
    ctr = lax.axis_index("ctr")
    idx_copy = pltpu.make_async_copy(idx_hbm, idx_ref, sems.at[SLOTS])
    idx_copy.start()
    rows[...] = jnp.zeros_like(rows)
    for c in range(N_CTR):
        counts[c] = 0
    idx_copy.wait()

    def note(i, most):
        owner = idx_ref[i] // c_rows
        count = counts[owner]
        listed[jnp.where(owner == ctr, count, n)] = i
        counts[owner] = count + 1
        return jnp.maximum(most, count + 1)

    most = lax.fori_loop(0, n, note, 0, unroll=8)
    rounds_ref[0] = (most + SLOTS - 1) // SLOTS
    done = 0 if first else round_ref[0] * SLOTS
    count = jnp.clip(counts[ctr] - done, 0, SLOTS)

    def copy_of(s):
        pos = idx_ref[listed[done + s]] - ctr * c_rows
        start = pl.multiple_of(pos // GROUP * GROUP, GROUP)
        return pltpu.make_async_copy(table_ref.at[pl.ds(start, GROUP)], groups.at[s], sems.at[s])

    def start(s, carry):
        copy_of(s).start()
        return carry

    def finish(s, carry):
        copy_of(s).wait()
        group = groups[s].astype(F32)
        place = lax.broadcasted_iota(jnp.int32, group.shape, 0)
        kept = jnp.where(place == idx_ref[listed[done + s]] % GROUP, group, 0.0)
        rows[pl.ds(s, 1), :] = jnp.sum(kept, axis=0, keepdims=True)
        return carry

    lax.fori_loop(0, count, start, 0)
    lax.fori_loop(0, count, finish, 0)
    packed = rows[...].astype(BF16)
    for c in range(N_CTR):
        out_ref[c] = packed


def pick(batch_idx, table, at_round=None):
    n = batch_idx.shape[0]
    first = at_round is None
    return pl.pallas_call(
        functools.partial(pick_kernel, first),
        in_specs=([] if first else [SMEM]) + [HBM, HBM],
        out_specs=[VMEM, SMEM],
        out_shape=[
            jax.ShapeDtypeStruct((N_CTR, SLOTS, D), BF16),
            jax.ShapeDtypeStruct((1,), jnp.int32),
        ],
        scratch_shapes=[
            pltpu.SMEM((n,), jnp.int32),
            pltpu.SMEM((N_CTR,), jnp.int32),
            pltpu.SMEM((n + 1,), jnp.int32),
            pltpu.VMEM((SLOTS, GROUP, D), BF16),
            pltpu.VMEM((SLOTS, D), F32),
            pltpu.SemaphoreType.DMA((SLOTS + 1,)),
        ],
        compiler_params=pltpu.CompilerParams(vmem_limit_bytes=8 * MIB),
        name="pick",
    )(
        *([] if first else [at_round]),
        in_hbm(batch_idx),
        in_hbm(table),
    )


def settled(idx_row, received, at_round, c_rows):
    n = idx_row.shape[1]
    owner_row = (idx_row // c_rows).astype(F32)
    i = lax.broadcasted_iota(jnp.int32, (n, n), 0)
    j = lax.broadcasted_iota(jnp.int32, (n, n), 1)
    owner = jnp.sum(jnp.where(i == j, owner_row, 0.0), axis=1, keepdims=True)
    before = (owner == owner_row) & (j < i)
    slot = jnp.sum(jnp.where(before, 1.0, 0.0), axis=1, keepdims=True) - at_round * SLOTS
    here = (slot >= 0.0) & (slot < SLOTS)
    place = jnp.where(here, owner * SLOTS + slot, -1.0)
    column = lax.broadcasted_iota(jnp.int32, (n, N_CTR * SLOTS), 1).astype(F32)
    chosen = jnp.where(column == place, 1.0, 0.0).astype(BF16)
    return jnp.dot(chosen, received, preferred_element_type=F32)


def settle_kernel(c_rows, round_ref, idx_ref, received_ref, before_ref, out_ref):
    at_round = round_ref[0].astype(F32)
    rows = settled(idx_ref[...], received_ref[...], at_round, c_rows)
    out_ref[...] = (rows + before_ref[...].astype(F32)).astype(BF16)


def settle(at_round, idx_row, received, before, c_rows):
    return pl.pallas_call(
        functools.partial(settle_kernel, c_rows),
        in_specs=[SMEM, VMEM, VMEM, VMEM],
        out_specs=VMEM,
        out_shape=jax.ShapeDtypeStruct(before.shape, BF16),
        compiler_params=pltpu.CompilerParams(vmem_limit_bytes=8 * MIB),
        name="settle",
    )(at_round, idx_row, received, before)


N_TILES = 8


def kern_kernel(
    idx_ref, received_in, more_in, nys_ref, table_ref, kern, kern16, local_ref,
    held, received_ref, more_ref, pts_ref, cross, sems
):
    n_tiles = sems.shape[0] - 2
    c_rows = held.shape[0]
    tile = c_rows // n_tiles

    def rows_of(i):
        return pl.ds(pl.multiple_of(i * tile, tile), tile)

    def copy_of(i):
        rows = rows_of(i)
        return pltpu.make_async_copy(table_ref.at[rows], held.at[rows], sems.at[i])

    received_copy = pltpu.make_async_copy(received_in, received_ref, sems.at[n_tiles])
    more_copy = pltpu.make_async_copy(more_in, more_ref, sems.at[n_tiles + 1])
    received_copy.start()
    more_copy.start()
    for i in range(n_tiles):
        copy_of(i).start()
    local_ref[...] = nys_ref[...] - lax.axis_index("ctr") * c_rows
    received_copy.wait()
    more_copy.wait()
    pts = settled(idx_ref[...], received_ref[...], 0.0, c_rows) + more_ref[...].astype(F32)
    pts_ref[...] = pts.astype(BF16)
    pts_sq = lax.dot_general(
        jnp.ones((8, D), F32), pts * pts, (((1,), (1,)), ((), ())),
        precision=lax.Precision.HIGHEST, preferred_element_type=F32,
    )[0:1]

    def multiply(i):
        copy_of(i).wait()
        cross[i % 2] = lax.dot_general(
            held[rows_of(i), :], pts_ref[...], (((1,), (1,)), ((), ())),
            preferred_element_type=F32,
        )

    def finish(i):
        wide = held[rows_of(i), :].astype(F32)
        row_sq = jnp.sum(wide * wide, axis=1, keepdims=True)
        k = jnp.exp(-SHARPNESS * (row_sq + pts_sq - 2.0 * cross[i % 2])).astype(BF16)
        kern[rows_of(i), :] = k.astype(F32)
        kern16[rows_of(i), :] = k

    def both(i, carry):
        multiply(i)
        finish(i - 1)
        return carry

    multiply(0)
    lax.fori_loop(1, n_tiles, both, 0)
    finish(n_tiles - 1)


def kernel_rows(idx_row, received, more, nystrom_idx, table):
    c_rows = table.shape[0]
    n = idx_row.shape[1]
    return pl.pallas_call(
        kern_kernel,
        in_specs=[VMEM, ANY, ANY, VMEM, HBM],
        out_specs=[VMEM, VMEM, VMEM],
        out_shape=[
            jax.ShapeDtypeStruct((c_rows, n), F32),
            jax.ShapeDtypeStruct((c_rows, n), BF16),
            jax.ShapeDtypeStruct(nystrom_idx.shape, jnp.int32),
        ],
        scratch_shapes=[
            pltpu.VMEM((c_rows, D), BF16),
            pltpu.VMEM(received.shape, BF16),
            pltpu.VMEM((n, D), BF16),
            pltpu.VMEM((n, D), BF16),
            pltpu.VMEM((2, c_rows // N_TILES, n), F32),
            pltpu.SemaphoreType.DMA((N_TILES + 2,)),
        ],
        compiler_params=pltpu.CompilerParams(vmem_limit_bytes=30 * MIB),
        cost_estimate=pl.CostEstimate(flops=10**10, bytes_accessed=24 * MIB, transcendentals=10**6),
        name="kernel_rows",
    )(
        idx_row, received, more, nystrom_idx, in_hbm(table)
    )


def comp_kernel(part, idx_ref, kern, eig_ref, *rest):
    if part:
        n_arrived = rest[-1].shape[0]
        before_ref, *arrived = rest[:1 + n_arrived]
        out_ref, *landed = rest[1 + n_arrived:-2]
        nys, sems = rest[-2:]
        copies = [pltpu.make_async_copy(x, y, sems.at[i]) for i, (x, y) in enumerate(zip(arrived, landed))]
        for copy in copies:
            copy.start()
    else:
        out_ref, nys = rest
    unroll = 32
    first, n = PARTS[part]

    def gather(j, carry):
        for u in range(unroll):
            m = j * unroll + u
            nys[pl.ds(m, 1), :] = kern[pl.ds(idx_ref[first + m], 1), :]
        return carry

    lax.fori_loop(0, n // unroll, gather, 0)
    comp = lax.dot_general(
        eig_ref[first:first + n, :], nys[...].astype(BF16), (((0,), (0,)), ((), ())),
        preferred_element_type=F32,
    )
    if part:
        comp += before_ref[...]
        for copy in copies:
            copy.wait()
    out_ref[...] = comp


def components(part, local_idx, kern, eigvecs, *rest):
    q = eigvecs.shape[1]
    n = kern.shape[1]
    arrived = rest[1:]
    return pl.pallas_call(
        functools.partial(comp_kernel, part),
        in_specs=[SMEM, VMEM, VMEM] + ([VMEM] + [ANY] * len(arrived) if part else []),
        out_specs=[VMEM] * (1 + len(arrived)),
        out_shape=[jax.ShapeDtypeStruct((q, n), F32)]
        + [jax.ShapeDtypeStruct(x.shape, x.dtype) for x in arrived],
        scratch_shapes=[pltpu.VMEM((PARTS[part][1], n), F32)]
        + ([pltpu.SemaphoreType.DMA((len(arrived),))] if part else []),
        compiler_params=pltpu.CompilerParams(vmem_limit_bytes=16 * MIB),
        cost_estimate=pl.CostEstimate(flops=3 * 10**9, bytes_accessed=6 * MIB, transcendentals=0),
        name="components",
    )(local_idx, kern, in_vmem(eigvecs), *rest)


def pred_kernel(comp_ref, kern16, *rest):
    coef_refs = rest[:8]
    out_ref, acc = rest[8:]
    coefs = jnp.concatenate([ref[...] for ref in coef_refs], axis=0)
    acc[...] = jnp.dot(coefs, kern16[...], preferred_element_type=F32)
    for c in range(N_CTR):
        out_ref[c, 0:16, :] = comp_ref[c * 16:(c + 1) * 16, :]
    bat = lax.axis_index("bat")
    z = bat // 2
    core = bat % 2
    for k in range(N_Z):
        for s in range(2):
            from_z = (z + N_Z - k) % N_Z
            from_core = core if s == 0 else 1 - core
            first = (2 * k + s) * 32
            for i in range(8):
                out_ref[from_core * 8 + i, pl.ds(16 + from_z * 4, 4), :] = acc[first + 4 * i:first + 4 * i + 4]


def predict(comp, kern16, pieces):
    return pl.pallas_call(
        pred_kernel,
        in_specs=[VMEM] * 10,
        out_specs=VMEM,
        out_shape=jax.ShapeDtypeStruct((N_CTR, 32, LANES), F32),
        scratch_shapes=[pltpu.VMEM((256, LANES), F32)],
        compiler_params=pltpu.CompilerParams(vmem_limit_bytes=16 * MIB),
        name="predict",
    )(comp, kern16, *[in_vmem(x) for x in pieces])


def split2(x):
    hi = x.astype(BF16)
    return hi, (x - hi.astype(F32)).astype(BF16)


def residual_of(ref, targets_ref, core, from_core, z):
    lanes = pl.ds(pl.multiple_of((2 * z + from_core) * LANES, LANES), LANES)
    pred = [ref[(core * 8 + i) * N_Z + z, 16:20, :] for i in range(8)]
    return lanes, jnp.concatenate(pred, axis=0) - targets_ref[:, lanes]


def projected(ref, z, residual):
    comp = jnp.concatenate([ref[c * N_Z + z, 0:16, :] for c in range(N_CTR)], axis=0)
    hi, lo = split2(comp)
    grad = residual.astype(BF16)
    dims = (((1,), (1,)), ((), ()))
    return lax.dot_general(grad, hi, dims, preferred_element_type=F32) + lax.dot_general(
        grad, lo, dims, preferred_element_type=F32
    )


def same_kernel(same_ref, targets_ref, proj_ref):
    core = lax.axis_index("bat") % 2
    proj = jnp.zeros(proj_ref.shape, F32)
    for z in range(N_Z):
        _, residual = residual_of(same_ref, targets_ref, core, core, z)
        proj += projected(same_ref, z, residual)
    proj_ref[...] = proj


def same_part(same, targets, q):
    return pl.pallas_call(
        same_kernel,
        in_specs=[VMEM, VMEM],
        out_specs=VMEM,
        out_shape=jax.ShapeDtypeStruct((targets.shape[0], q), F32),
        compiler_params=pltpu.CompilerParams(vmem_limit_bytes=16 * MIB),
        name="same_part",
    )(same, targets)


def final_kernel(same_ref, other_ref, proj_ref, targets_ref, corr_ref, eig_ref, res_ref, upd_ref):
    core = lax.axis_index("bat") % 2
    proj = proj_ref[...]
    for z in range(N_Z):
        lanes, residual = residual_of(same_ref, targets_ref, core, core, z)
        res_ref[:, lanes] = residual
        lanes, residual = residual_of(other_ref, targets_ref, core, 1 - core, z)
        res_ref[:, lanes] = residual
        proj += projected(other_ref, z, residual)
    scaled = jnp.concatenate(split2(proj * corr_ref[...]), axis=0)
    upd = lax.dot_general(
        scaled, eig_ref[...], (((1,), (1,)), ((), ())), preferred_element_type=F32
    )
    upd_ref[...] = upd[0:32] + upd[32:64]


def final(same, other, proj, targets, correction, eigvecs):
    cols, n = targets.shape
    m_rows, q = eigvecs.shape
    return pl.pallas_call(
        final_kernel,
        in_specs=[VMEM] * 6,
        out_specs=[VMEM, VMEM],
        out_shape=[
            jax.ShapeDtypeStruct((cols, n), F32),
            jax.ShapeDtypeStruct((cols, m_rows), F32),
        ],
        compiler_params=pltpu.CompilerParams(vmem_limit_bytes=16 * MIB),
        name="final",
    )(same, other, proj, targets, correction, in_vmem(eigvecs))


def per_device(table, coefs, targets, eigvecs, correction, batch_idx, nystrom_idx):
    c_rows = table.shape[0]
    picked, rounds = pick(batch_idx, table)
    idx_row = batch_idx.reshape(1, -1)

    def further(state):
        at_round, more = state
        sent, _ = pick(batch_idx, table, at_round.reshape(1))
        got = lax.all_to_all(sent, "ctr", 0, 0).reshape(-1, D)
        return at_round + 1, settle(at_round.reshape(1), idx_row, got, more, c_rows)

    none = jnp.zeros((batch_idx.shape[0], D), BF16)
    _, more = lax.while_loop(lambda state: state[0] < rounds[0], further, (jnp.int32(1), none))
    picked, more, own = lax.optimization_barrier((picked, more, coefs.T))
    from_z = [lax.ppermute(own, "bat", z_shift(k)) if k else own for k in range(N_Z)]
    received = lax.all_to_all(picked, "ctr", 0, 0).reshape(-1, D)

    kern, kern16, local_idx = kernel_rows(
        idx_row, received, more, nystrom_idx.reshape(-1, LANES), table
    )
    local_idx = local_idx.reshape(-1)
    comp, = components(0, local_idx, kern, eigvecs)
    comp, late, *arrived = lax.optimization_barrier((comp, *from_z))
    own_swapped, *swapped = [lax.ppermute(x, "bat", SWAP) for x in (late, *arrived)]
    comp, *arrived = components(1, local_idx, kern, eigvecs, comp, *arrived)
    pieces = [x for pair in zip((own, *arrived), (own_swapped, *swapped)) for x in pair]
    partial = predict(comp, kern16, pieces)
    mine = jnp.sum(lax.all_to_all(partial, "ctr", 0, 0), axis=0)
    comp = jnp.broadcast_to(mine[None, :16], (N_Z, 16, LANES))
    pred = jnp.pad(mine[16:].reshape(N_Z, 4, LANES), ((0, 0), (0, 4), (0, 0)))
    sent = jnp.concatenate([comp, pred], axis=1)
    sent = jnp.broadcast_to(sent[None], (N_CTR,) + sent.shape).reshape((-1,) + sent.shape[1:])
    same = lax.all_to_all(sent, ("ctr", "bat"), 0, 0, axis_index_groups=SAME_CORE)
    other = lax.ppermute(same, "bat", SWAP)
    proj = same_part(same, targets.T, eigvecs.shape[1])
    residual, update = final(same, other, proj, targets.T, correction[None], eigvecs)
    return residual.T, update.T


def solution(mesh):
    return jax.shard_map(
        per_device,
        mesh=mesh,
        in_specs=(
            P("ctr", None),
            P("ctr", "bat"),
            P(None, "bat"),
            P("ctr", None),
            P(),
            P("bat"),
            P("ctr"),
        ),
        out_specs=(P(None, "bat"), P("ctr", "bat")),
        check_vma=False,
    )
```

```python
import functools

import jax
import jax.numpy as jnp
from jax import lax
from jax.experimental import pallas as pl
from jax.experimental.pallas import tpu as pltpu
from jax.sharding import PartitionSpec as P

D = 1024
SHARPNESS = 4.0 / D
N_CTR = 16
N_Z = 4
LANES = 128
GROUP = 16
SLOTS = 24
PARTS = ((0, 2048), (2048, 2048))
MIB = 2**20
F32 = jnp.float32
BF16 = jnp.bfloat16
SMEM = pl.BlockSpec(memory_space=pltpu.SMEM)
VMEM = pl.BlockSpec(memory_space=pltpu.VMEM)
HBM = pl.BlockSpec(memory_space=pltpu.HBM)
ANY = pl.BlockSpec(memory_space=pl.ANY)
SWAP = [(i, i ^ 1) for i in range(2 * N_Z)]
SAME_CORE = [[c * 8 + z * 2 + k for c in range(N_CTR) for z in range(N_Z)] for k in range(2)]


def z_shift(k):
    return [(z * 2 + c, (z + k) % N_Z * 2 + c) for z in range(N_Z) for c in range(2)]


def in_vmem(x):
    return pltpu.with_memory_space_constraint(x, pltpu.VMEM)


def in_hbm(x):
    return pltpu.with_memory_space_constraint(x, pltpu.HBM)


def pick_kernel(first, *refs):
    done = 0 if first else refs[0][0] * SLOTS
    idx_hbm, table_ref, out_ref, idx_ref, listed, groups, rows, sems = refs[0 if first else 1:]
    n = idx_ref.shape[0]
    c_rows = table_ref.shape[0]
    first_row = lax.axis_index("ctr") * c_rows
    idx_copy = pltpu.make_async_copy(idx_hbm, idx_ref, sems.at[SLOTS])
    idx_copy.start()
    rows[...] = jnp.zeros_like(rows)
    idx_copy.wait()

    def note(i, count):
        pos = idx_ref[i] - first_row
        listed[count] = pos
        return count + jnp.where((pos >= 0) & (pos < c_rows), 1, 0)

    count = jnp.clip(lax.fori_loop(0, n, note, 0, unroll=16) - done, 0, SLOTS)

    def copy_of(s):
        start = pl.multiple_of(listed[done + s] // GROUP * GROUP, GROUP)
        return pltpu.make_async_copy(table_ref.at[pl.ds(start, GROUP)], groups.at[s], sems.at[s])

    def start(s, carry):
        copy_of(s).start()
        return carry

    def finish(s, carry):
        copy_of(s).wait()
        group = groups[s].astype(F32)
        place = lax.broadcasted_iota(jnp.int32, group.shape, 0)
        kept = jnp.where(place == listed[done + s] % GROUP, group, 0.0)
        rows[pl.ds(s, 1), :] = jnp.sum(kept, axis=0, keepdims=True)
        return carry

    lax.fori_loop(0, count, start, 0)
    lax.fori_loop(0, count, finish, 0)
    packed = rows[...].astype(BF16)
    for c in range(N_CTR):
        out_ref[c] = packed


def pick(batch_idx, table, at_round=None):
    n = batch_idx.shape[0]
    first = at_round is None
    return pl.pallas_call(
        functools.partial(pick_kernel, first),
        in_specs=([] if first else [SMEM]) + [HBM, HBM],
        out_specs=VMEM,
        out_shape=jax.ShapeDtypeStruct((N_CTR, SLOTS, D), BF16),
        scratch_shapes=[
            pltpu.SMEM((n,), jnp.int32),
            pltpu.SMEM((n + 1,), jnp.int32),
            pltpu.VMEM((SLOTS, GROUP, D), BF16),
            pltpu.VMEM((SLOTS, D), F32),
            pltpu.SemaphoreType.DMA((SLOTS + 1,)),
        ],
        compiler_params=pltpu.CompilerParams(vmem_limit_bytes=8 * MIB),
        name="pick",
    )(*([] if first else [at_round]), in_hbm(batch_idx), in_hbm(table))


def owners(idx_row, c_rows):
    n = idx_row.shape[1]
    row = (idx_row // c_rows).astype(F32)
    i = lax.broadcasted_iota(jnp.int32, (n, n), 0)
    j = lax.broadcasted_iota(jnp.int32, (n, n), 1)
    column = jnp.sum(jnp.where(i == j, row, 0.0), axis=1, keepdims=True)
    return column, column == row, j < i


def count_kernel(c_rows, idx_ref, rounds_ref):
    _, alike, _ = owners(idx_ref[...], c_rows)
    most = jnp.max(jnp.sum(jnp.where(alike, 1.0, 0.0), axis=1, keepdims=True))
    rounds_ref[0] = (most.astype(jnp.int32) + SLOTS - 1) // SLOTS


def count_rounds(idx_row, c_rows):
    return pl.pallas_call(
        functools.partial(count_kernel, c_rows),
        in_specs=[VMEM],
        out_specs=SMEM,
        out_shape=jax.ShapeDtypeStruct((1,), jnp.int32),
        cost_estimate=pl.CostEstimate(flops=10**9, bytes_accessed=MIB, transcendentals=0),
        name="count_rounds",
    )(idx_row)


def settled(idx_row, received, at_round, c_rows):
    n = idx_row.shape[1]
    owner, alike, earlier = owners(idx_row, c_rows)
    before = alike & earlier
    slot = jnp.sum(jnp.where(before, 1.0, 0.0), axis=1, keepdims=True) - at_round * SLOTS
    here = (slot >= 0.0) & (slot < SLOTS)
    place = jnp.where(here, owner * SLOTS + slot, -1.0)
    column = lax.broadcasted_iota(jnp.int32, (n, N_CTR * SLOTS), 1).astype(F32)
    chosen = jnp.where(column == place, 1.0, 0.0).astype(BF16)
    return jnp.dot(chosen, received, preferred_element_type=F32)


def settle_kernel(c_rows, round_ref, idx_ref, received_ref, before_ref, out_ref):
    at_round = round_ref[0].astype(F32)
    rows = settled(idx_ref[...], received_ref[...], at_round, c_rows)
    out_ref[...] = (rows + before_ref[...].astype(F32)).astype(BF16)


def settle(at_round, idx_row, received, before, c_rows):
    return pl.pallas_call(
        functools.partial(settle_kernel, c_rows),
        in_specs=[SMEM, VMEM, VMEM, VMEM],
        out_specs=VMEM,
        out_shape=jax.ShapeDtypeStruct(before.shape, BF16),
        compiler_params=pltpu.CompilerParams(vmem_limit_bytes=8 * MIB),
        name="settle",
    )(at_round, idx_row, received, before)


N_TILES = 8


def kern_kernel(
    idx_ref, received_in, more_in, nys_ref, table_ref, kern, kern16, local_ref,
    held, received_ref, more_ref, pts_ref, cross, sems
):
    n_tiles = sems.shape[0] - 2
    c_rows = held.shape[0]
    tile = c_rows // n_tiles

    def rows_of(i):
        return pl.ds(pl.multiple_of(i * tile, tile), tile)

    def copy_of(i):
        rows = rows_of(i)
        return pltpu.make_async_copy(table_ref.at[rows], held.at[rows], sems.at[i])

    received_copy = pltpu.make_async_copy(received_in, received_ref, sems.at[n_tiles])
    more_copy = pltpu.make_async_copy(more_in, more_ref, sems.at[n_tiles + 1])
    received_copy.start()
    more_copy.start()
    for i in range(n_tiles):
        copy_of(i).start()
    local_ref[...] = nys_ref[...] - lax.axis_index("ctr") * c_rows
    received_copy.wait()
    more_copy.wait()
    pts = settled(idx_ref[...], received_ref[...], 0.0, c_rows) + more_ref[...].astype(F32)
    pts_ref[...] = pts.astype(BF16)
    n = pts.shape[0]
    on_diagonal = lax.broadcasted_iota(jnp.int32, (n, n), 0) == lax.broadcasted_iota(jnp.int32, (n, n), 1)
    sums = jnp.sum(pts * pts, axis=1, keepdims=True)
    pts_sq = jnp.sum(jnp.where(on_diagonal, sums, 0.0), axis=0, keepdims=True)

    def multiply(i):
        copy_of(i).wait()
        cross[i % 2] = lax.dot_general(
            held[rows_of(i), :], pts_ref[...], (((1,), (1,)), ((), ())),
            preferred_element_type=F32,
        )

    def finish(i):
        wide = held[rows_of(i), :].astype(F32)
        row_sq = jnp.sum(wide * wide, axis=1, keepdims=True)
        k = jnp.exp(-SHARPNESS * (row_sq + pts_sq - 2.0 * cross[i % 2])).astype(BF16)
        kern[rows_of(i), :] = k.astype(F32)
        kern16[rows_of(i), :] = k

    def both(i, carry):
        multiply(i)
        finish(i - 1)
        return carry

    multiply(0)
    lax.fori_loop(1, n_tiles, both, 0)
    finish(n_tiles - 1)


def kernel_rows(idx_row, received, more, nystrom_idx, table):
    c_rows = table.shape[0]
    n = idx_row.shape[1]
    return pl.pallas_call(
        kern_kernel,
        in_specs=[VMEM, ANY, ANY, VMEM, HBM],
        out_specs=[VMEM, VMEM, VMEM],
        out_shape=[
            jax.ShapeDtypeStruct((c_rows, n), F32),
            jax.ShapeDtypeStruct((c_rows, n), BF16),
            jax.ShapeDtypeStruct(nystrom_idx.shape, jnp.int32),
        ],
        scratch_shapes=[
            pltpu.VMEM((c_rows, D), BF16),
            pltpu.VMEM(received.shape, BF16),
            pltpu.VMEM((n, D), BF16),
            pltpu.VMEM((n, D), BF16),
            pltpu.VMEM((2, c_rows // N_TILES, n), F32),
            pltpu.SemaphoreType.DMA((N_TILES + 2,)),
        ],
        compiler_params=pltpu.CompilerParams(vmem_limit_bytes=30 * MIB),
        cost_estimate=pl.CostEstimate(flops=10**10, bytes_accessed=24 * MIB, transcendentals=10**6),
        name="kernel_rows",
    )(
        idx_row, received, more, nystrom_idx, in_hbm(table)
    )


def comp_kernel(part, idx_ref, kern, eig_ref, *rest):
    if part:
        n_arrived = rest[-1].shape[0]
        before_ref, *arrived = rest[:1 + n_arrived]
        out_ref, *landed = rest[1 + n_arrived:-2]
        nys, sems = rest[-2:]
        copies = [pltpu.make_async_copy(x, y, sems.at[i]) for i, (x, y) in enumerate(zip(arrived, landed))]
        for copy in copies:
            copy.start()
    else:
        out_ref, nys = rest
    unroll = 64
    first, n = PARTS[part]

    def gather(j, carry):
        for u in range(unroll):
            m = j * unroll + u
            nys[pl.ds(m, 1), :] = kern[pl.ds(idx_ref[first + m], 1), :]
        return carry

    lax.fori_loop(0, n // unroll, gather, 0)
    comp = lax.dot_general(
        eig_ref[first:first + n, :], nys[...].astype(BF16), (((0,), (0,)), ((), ())),
        preferred_element_type=F32,
    )
    if part:
        comp += before_ref[...]
        for copy in copies:
            copy.wait()
    out_ref[...] = comp


def components(part, local_idx, kern, eigvecs, *rest):
    q = eigvecs.shape[1]
    n = kern.shape[1]
    arrived = rest[1:]
    return pl.pallas_call(
        functools.partial(comp_kernel, part),
        in_specs=[SMEM, VMEM, VMEM] + ([VMEM] + [ANY] * len(arrived) if part else []),
        out_specs=[VMEM] * (1 + len(arrived)),
        out_shape=[jax.ShapeDtypeStruct((q, n), F32)]
        + [jax.ShapeDtypeStruct(x.shape, x.dtype) for x in arrived],
        scratch_shapes=[pltpu.VMEM((PARTS[part][1], n), F32)]
        + ([pltpu.SemaphoreType.DMA((len(arrived),))] if part else []),
        compiler_params=pltpu.CompilerParams(vmem_limit_bytes=16 * MIB),
        cost_estimate=pl.CostEstimate(flops=3 * 10**9, bytes_accessed=6 * MIB, transcendentals=0),
        name="components",
    )(local_idx, kern, in_vmem(eigvecs), *rest)


def pred_kernel(comp_ref, kern16, *rest):
    coef_refs = rest[:8]
    out_ref, acc = rest[8:]
    coefs = jnp.concatenate([ref[...] for ref in coef_refs], axis=0)
    acc[...] = jnp.dot(coefs, kern16[...], preferred_element_type=F32)
    for c in range(N_CTR):
        out_ref[c, 0:16, :] = comp_ref[c * 16:(c + 1) * 16, :]
    bat = lax.axis_index("bat")
    z = bat // 2
    core = bat % 2
    for k in range(N_Z):
        for s in range(2):
            from_z = (z + N_Z - k) % N_Z
            from_core = core if s == 0 else 1 - core
            first = (2 * k + s) * 32
            for i in range(8):
                out_ref[from_core * 8 + i, pl.ds(16 + from_z * 4, 4), :] = acc[first + 4 * i:first + 4 * i + 4]


def predict(comp, kern16, pieces):
    return pl.pallas_call(
        pred_kernel,
        in_specs=[VMEM] * 10,
        out_specs=VMEM,
        out_shape=jax.ShapeDtypeStruct((N_CTR, 32, LANES), F32),
        scratch_shapes=[pltpu.VMEM((256, LANES), F32)],
        compiler_params=pltpu.CompilerParams(vmem_limit_bytes=16 * MIB),
        name="predict",
    )(comp, kern16, *[in_vmem(x) for x in pieces])


def split2(x):
    hi = x.astype(BF16)
    return hi, (x - hi.astype(F32)).astype(BF16)


def residual_of(ref, targets_ref, core, from_core, z):
    lanes = pl.ds(pl.multiple_of((2 * z + from_core) * LANES, LANES), LANES)
    pred = [ref[(core * 8 + i) * N_Z + z, 16:20, :] for i in range(8)]
    return lanes, jnp.concatenate(pred, axis=0) - targets_ref[:, lanes]


def projected(ref, z, residual):
    comp = jnp.concatenate([ref[c * N_Z + z, 0:16, :] for c in range(N_CTR)], axis=0)
    hi, lo = split2(comp)
    grad = residual.astype(BF16)
    dims = (((1,), (1,)), ((), ()))
    return lax.dot_general(grad, hi, dims, preferred_element_type=F32) + lax.dot_general(
        grad, lo, dims, preferred_element_type=F32
    )


def same_kernel(same_ref, targets_ref, proj_ref):
    core = lax.axis_index("bat") % 2
    proj = jnp.zeros(proj_ref.shape, F32)
    for z in range(N_Z):
        _, residual = residual_of(same_ref, targets_ref, core, core, z)
        proj += projected(same_ref, z, residual)
    proj_ref[...] = proj


def same_part(same, targets, q):
    return pl.pallas_call(
        same_kernel,
        in_specs=[VMEM, VMEM],
        out_specs=VMEM,
        out_shape=jax.ShapeDtypeStruct((targets.shape[0], q), F32),
        compiler_params=pltpu.CompilerParams(vmem_limit_bytes=16 * MIB),
        name="same_part",
    )(same, targets)


def final_kernel(same_ref, other_ref, proj_ref, targets_ref, corr_ref, eig_ref, res_ref, upd_ref):
    core = lax.axis_index("bat") % 2
    proj = proj_ref[...]
    for z in range(N_Z):
        lanes, residual = residual_of(same_ref, targets_ref, core, core, z)
        res_ref[:, lanes] = residual
        lanes, residual = residual_of(other_ref, targets_ref, core, 1 - core, z)
        res_ref[:, lanes] = residual
        proj += projected(other_ref, z, residual)
    scaled = jnp.concatenate(split2(proj * corr_ref[...]), axis=0)
    upd = lax.dot_general(
        scaled, eig_ref[...], (((1,), (1,)), ((), ())), preferred_element_type=F32
    )
    upd_ref[...] = upd[0:32] + upd[32:64]


def final(same, other, proj, targets, correction, eigvecs):
    cols, n = targets.shape
    m_rows, q = eigvecs.shape
    return pl.pallas_call(
        final_kernel,
        in_specs=[VMEM] * 6,
        out_specs=[VMEM, VMEM],
        out_shape=[
            jax.ShapeDtypeStruct((cols, n), F32),
            jax.ShapeDtypeStruct((cols, m_rows), F32),
        ],
        compiler_params=pltpu.CompilerParams(vmem_limit_bytes=16 * MIB),
        name="final",
    )(same, other, proj, targets, correction, in_vmem(eigvecs))


def per_device(table, coefs, targets, eigvecs, correction, batch_idx, nystrom_idx):
    c_rows = table.shape[0]
    idx_row = batch_idx.reshape(1, -1)
    picked = pick(batch_idx, table)
    picked, idx_row, own = lax.optimization_barrier((picked, idx_row, coefs.T))
    from_z = [lax.ppermute(own, "bat", z_shift(k)) if k else own for k in range(N_Z)]
    received = lax.all_to_all(picked, "ctr", 0, 0).reshape(-1, D)
    rounds = count_rounds(idx_row, c_rows)
    received, rounds = lax.optimization_barrier((received, rounds))

    def further(state):
        at_round, more = state
        sent = pick(batch_idx, table, at_round.reshape(1))
        got = lax.all_to_all(sent, "ctr", 0, 0).reshape(-1, D)
        return at_round + 1, settle(at_round.reshape(1), idx_row, got, more, c_rows)

    none = jnp.zeros((batch_idx.shape[0], D), BF16)
    _, more = lax.while_loop(lambda state: state[0] < rounds[0], further, (jnp.int32(1), none))
    kern, kern16, local_idx = kernel_rows(
        idx_row, received, more, nystrom_idx.reshape(-1, LANES), table
    )
    local_idx = local_idx.reshape(-1)
    comp, = components(0, local_idx, kern, eigvecs)
    comp, late, *arrived = lax.optimization_barrier((comp, *from_z))
    own_swapped, *swapped = [lax.ppermute(x, "bat", SWAP) for x in (late, *arrived)]
    comp, *arrived = components(1, local_idx, kern, eigvecs, comp, *arrived)
    pieces = [x for pair in zip((own, *arrived), (own_swapped, *swapped)) for x in pair]
    partial = predict(comp, kern16, pieces)
    mine = jnp.sum(lax.all_to_all(partial, "ctr", 0, 0), axis=0)
    comp = jnp.broadcast_to(mine[None, :16], (N_Z, 16, LANES))
    pred = jnp.pad(mine[16:].reshape(N_Z, 4, LANES), ((0, 0), (0, 4), (0, 0)))
    sent = jnp.concatenate([comp, pred], axis=1)
    sent = jnp.broadcast_to(sent[None], (N_CTR,) + sent.shape).reshape((-1,) + sent.shape[1:])
    same = lax.all_to_all(sent, ("ctr", "bat"), 0, 0, axis_index_groups=SAME_CORE)
    other = lax.ppermute(same, "bat", SWAP)
    proj = same_part(same, targets.T, eigvecs.shape[1])
    residual, update = final(same, other, proj, targets.T, correction[None], eigvecs)
    return residual.T, update.T


def solution(mesh):
    return jax.shard_map(
        per_device,
        mesh=mesh,
        in_specs=(
            P("ctr", None),
            P("ctr", "bat"),
            P(None, "bat"),
            P("ctr", None),
            P(),
            P("bat"),
            P("ctr"),
        ),
        out_specs=(P(None, "bat"), P("ctr", "bat")),
        check_vma=False,
    )
```

```python
import functools

import jax
import jax.numpy as jnp
from jax import lax
from jax.experimental import pallas as pl
from jax.experimental.pallas import tpu as pltpu
from jax.sharding import PartitionSpec as P

D = 1024
SHARPNESS = 4.0 / D
N_CTR = 16
N_Z = 4
SHIFTS = (0, 1, 3, 2)
LANES = 128
GROUP = 16
SLOTS = 24
PARTS = ((0, 2048), (2048, 2048))
MIB = 2**20
F32 = jnp.float32
BF16 = jnp.bfloat16
SMEM = pl.BlockSpec(memory_space=pltpu.SMEM)
VMEM = pl.BlockSpec(memory_space=pltpu.VMEM)
HBM = pl.BlockSpec(memory_space=pltpu.HBM)
ANY = pl.BlockSpec(memory_space=pl.ANY)
SWAP = [(i, i ^ 1) for i in range(2 * N_Z)]
SAME_CORE = [[c * 8 + z * 2 + k for c in range(N_CTR) for z in range(N_Z)] for k in range(2)]


def z_shift(k):
    return [(z * 2 + c, (z + k) % N_Z * 2 + c) for z in range(N_Z) for c in range(2)]


def in_vmem(x):
    return pltpu.with_memory_space_constraint(x, pltpu.VMEM)


def in_hbm(x):
    return pltpu.with_memory_space_constraint(x, pltpu.HBM)


def pick_kernel(first, *refs):
    done = 0 if first else refs[0][0] * SLOTS
    idx_hbm, table_ref, out_ref, idx_ref, listed, groups, rows, sems = refs[0 if first else 1:]
    n = idx_ref.shape[0]
    c_rows = table_ref.shape[0]
    first_row = lax.axis_index("ctr") * c_rows
    idx_copy = pltpu.make_async_copy(idx_hbm, idx_ref, sems.at[SLOTS])
    idx_copy.start()
    rows[...] = jnp.zeros_like(rows)
    idx_copy.wait()

    def note(i, count):
        pos = idx_ref[i] - first_row
        listed[count] = pos
        return count + jnp.where((pos >= 0) & (pos < c_rows), 1, 0)

    count = jnp.clip(lax.fori_loop(0, n, note, 0, unroll=16) - done, 0, SLOTS)

    def copy_of(s):
        start = pl.multiple_of(listed[done + s] // GROUP * GROUP, GROUP)
        return pltpu.make_async_copy(table_ref.at[pl.ds(start, GROUP)], groups.at[s], sems.at[s])

    def start(s, carry):
        copy_of(s).start()
        return carry

    def finish(s, carry):
        copy_of(s).wait()
        group = groups[s].astype(F32)
        place = lax.broadcasted_iota(jnp.int32, group.shape, 0)
        kept = jnp.where(place == listed[done + s] % GROUP, group, 0.0)
        rows[pl.ds(s, 1), :] = jnp.sum(kept, axis=0, keepdims=True)
        return carry

    lax.fori_loop(0, count, start, 0)
    lax.fori_loop(0, count, finish, 0)
    packed = rows[...].astype(BF16)
    for c in range(N_CTR):
        out_ref[c] = packed


def pick(batch_idx, table, at_round=None):
    n = batch_idx.shape[0]
    first = at_round is None
    return pl.pallas_call(
        functools.partial(pick_kernel, first),
        in_specs=([] if first else [SMEM]) + [HBM, HBM],
        out_specs=VMEM,
        out_shape=jax.ShapeDtypeStruct((N_CTR, SLOTS, D), BF16),
        scratch_shapes=[
            pltpu.SMEM((n,), jnp.int32),
            pltpu.SMEM((n + 1,), jnp.int32),
            pltpu.VMEM((SLOTS, GROUP, D), BF16),
            pltpu.VMEM((SLOTS, D), F32),
            pltpu.SemaphoreType.DMA((SLOTS + 1,)),
        ],
        compiler_params=pltpu.CompilerParams(vmem_limit_bytes=8 * MIB),
        name="pick",
    )(*([] if first else [at_round]), in_hbm(batch_idx), in_hbm(table))


def owners(idx_row, c_rows):
    n = idx_row.shape[1]
    row = (idx_row // c_rows).astype(F32)
    i = lax.broadcasted_iota(jnp.int32, (n, n), 0)
    j = lax.broadcasted_iota(jnp.int32, (n, n), 1)
    column = jnp.sum(jnp.where(i == j, row, 0.0), axis=1, keepdims=True)
    return column, column == row, j < i


def count_kernel(c_rows, idx_ref, rounds_ref):
    _, alike, _ = owners(idx_ref[...], c_rows)
    most = jnp.max(jnp.sum(jnp.where(alike, 1.0, 0.0), axis=1, keepdims=True))
    rounds_ref[0] = (most.astype(jnp.int32) + SLOTS - 1) // SLOTS


def count_rounds(idx_row, c_rows):
    return pl.pallas_call(
        functools.partial(count_kernel, c_rows),
        in_specs=[VMEM],
        out_specs=SMEM,
        out_shape=jax.ShapeDtypeStruct((1,), jnp.int32),
        cost_estimate=pl.CostEstimate(flops=10**9, bytes_accessed=MIB, transcendentals=0),
        name="count_rounds",
    )(idx_row)


def settled(idx_row, received, at_round, c_rows):
    n = idx_row.shape[1]
    owner, alike, earlier = owners(idx_row, c_rows)
    before = alike & earlier
    slot = jnp.sum(jnp.where(before, 1.0, 0.0), axis=1, keepdims=True) - at_round * SLOTS
    here = (slot >= 0.0) & (slot < SLOTS)
    place = jnp.where(here, owner * SLOTS + slot, -1.0)
    column = lax.broadcasted_iota(jnp.int32, (n, N_CTR * SLOTS), 1).astype(F32)
    chosen = jnp.where(column == place, 1.0, 0.0).astype(BF16)
    return jnp.dot(chosen, received, preferred_element_type=F32)


def settle_kernel(c_rows, round_ref, idx_ref, received_ref, before_hbm, out_hbm, rows_ref, sem):
    copy_in = pltpu.make_async_copy(before_hbm, rows_ref, sem)
    copy_in.start()
    rows = settled(idx_ref[...], received_ref[...], round_ref[0].astype(F32), c_rows)
    copy_in.wait()
    rows_ref[...] = (rows + rows_ref[...].astype(F32)).astype(BF16)
    copy_out = pltpu.make_async_copy(rows_ref, out_hbm, sem)
    copy_out.start()
    copy_out.wait()


def settle(at_round, idx_row, received, before, c_rows):
    return pl.pallas_call(
        functools.partial(settle_kernel, c_rows),
        in_specs=[SMEM, VMEM, VMEM, HBM],
        out_specs=HBM,
        out_shape=jax.ShapeDtypeStruct(before.shape, BF16),
        scratch_shapes=[pltpu.VMEM(before.shape, BF16), pltpu.SemaphoreType.DMA(())],
        compiler_params=pltpu.CompilerParams(vmem_limit_bytes=8 * MIB),
        name="settle",
    )(at_round, idx_row, received, in_hbm(before))


N_TILES = 8


def kern_kernel(
    idx_ref, received_in, more_in, nys_ref, table_ref, kern, kern16, local_ref,
    held, received_ref, more_ref, pts_ref, cross, sems
):
    n_tiles = sems.shape[0] - 2
    c_rows = held.shape[0]
    tile = c_rows // n_tiles

    def rows_of(i):
        return pl.ds(pl.multiple_of(i * tile, tile), tile)

    def copy_of(i):
        rows = rows_of(i)
        return pltpu.make_async_copy(table_ref.at[rows], held.at[rows], sems.at[i])

    received_copy = pltpu.make_async_copy(received_in, received_ref, sems.at[n_tiles])
    more_copy = pltpu.make_async_copy(more_in, more_ref, sems.at[n_tiles + 1])
    received_copy.start()
    more_copy.start()
    for i in range(n_tiles):
        copy_of(i).start()
    local_ref[...] = nys_ref[...] - lax.axis_index("ctr") * c_rows
    received_copy.wait()
    more_copy.wait()
    pts = settled(idx_ref[...], received_ref[...], 0.0, c_rows) + more_ref[...].astype(F32)
    pts_ref[...] = pts.astype(BF16)
    n = pts.shape[0]
    on_diagonal = lax.broadcasted_iota(jnp.int32, (n, n), 0) == lax.broadcasted_iota(jnp.int32, (n, n), 1)
    sums = jnp.sum(pts * pts, axis=1, keepdims=True)
    pts_sq = jnp.sum(jnp.where(on_diagonal, sums, 0.0), axis=0, keepdims=True)

    def multiply(i):
        copy_of(i).wait()
        cross[i % 2] = lax.dot_general(
            held[rows_of(i), :], pts_ref[...], (((1,), (1,)), ((), ())),
            preferred_element_type=F32,
        )

    def finish(i):
        wide = held[rows_of(i), :].astype(F32)
        row_sq = jnp.sum(wide * wide, axis=1, keepdims=True)
        k = jnp.exp(-SHARPNESS * (row_sq + pts_sq - 2.0 * cross[i % 2])).astype(BF16)
        kern[rows_of(i), :] = k.astype(F32)
        kern16[rows_of(i), :] = k

    def both(i, carry):
        multiply(i)
        finish(i - 1)
        return carry

    multiply(0)
    lax.fori_loop(1, n_tiles, both, 0)
    finish(n_tiles - 1)


def kernel_rows(idx_row, received, more, nystrom_idx, table):
    c_rows = table.shape[0]
    n = idx_row.shape[1]
    return pl.pallas_call(
        kern_kernel,
        in_specs=[VMEM, ANY, ANY, VMEM, HBM],
        out_specs=[VMEM, VMEM, VMEM],
        out_shape=[
            jax.ShapeDtypeStruct((c_rows, n), F32),
            jax.ShapeDtypeStruct((c_rows, n), BF16),
            jax.ShapeDtypeStruct(nystrom_idx.shape, jnp.int32),
        ],
        scratch_shapes=[
            pltpu.VMEM((c_rows, D), BF16),
            pltpu.VMEM(received.shape, BF16),
            pltpu.VMEM((n, D), BF16),
            pltpu.VMEM((n, D), BF16),
            pltpu.VMEM((2, c_rows // N_TILES, n), F32),
            pltpu.SemaphoreType.DMA((N_TILES + 2,)),
        ],
        compiler_params=pltpu.CompilerParams(vmem_limit_bytes=30 * MIB),
        cost_estimate=pl.CostEstimate(flops=10**10, bytes_accessed=24 * MIB, transcendentals=10**6),
        name="kernel_rows",
    )(
        idx_row, received, more, nystrom_idx, in_hbm(table)
    )


def comp_kernel(part, idx_ref, kern, eig_ref, *rest):
    if part:
        n_arrived = rest[-1].shape[0]
        before_ref, *arrived = rest[:1 + n_arrived]
        out_ref, *landed = rest[1 + n_arrived:-2]
        nys, sems = rest[-2:]
        copies = [pltpu.make_async_copy(x, y, sems.at[i]) for i, (x, y) in enumerate(zip(arrived, landed))]
        for copy in copies:
            copy.start()
    else:
        out_ref, nys = rest
    unroll = 64
    first, n = PARTS[part]

    def gather(j, carry):
        for u in range(unroll):
            m = j * unroll + u
            nys[pl.ds(m, 1), :] = kern[pl.ds(idx_ref[first + m], 1), :]
        return carry

    lax.fori_loop(0, n // unroll, gather, 0)
    comp = lax.dot_general(
        eig_ref[first:first + n, :], nys[...].astype(BF16), (((0,), (0,)), ((), ())),
        preferred_element_type=F32,
    )
    if part:
        comp += before_ref[...]
        for copy in copies:
            copy.wait()
    out_ref[...] = comp


def components(part, local_idx, kern, eigvecs, *rest):
    q = eigvecs.shape[1]
    n = kern.shape[1]
    arrived = rest[1:]
    return pl.pallas_call(
        functools.partial(comp_kernel, part),
        in_specs=[SMEM, VMEM, VMEM] + ([VMEM] + [ANY] * len(arrived) if part else []),
        out_specs=[VMEM] * (1 + len(arrived)),
        out_shape=[jax.ShapeDtypeStruct((q, n), F32)]
        + [jax.ShapeDtypeStruct(x.shape, x.dtype) for x in arrived],
        scratch_shapes=[pltpu.VMEM((PARTS[part][1], n), F32)]
        + ([pltpu.SemaphoreType.DMA((len(arrived),))] if part else []),
        compiler_params=pltpu.CompilerParams(vmem_limit_bytes=16 * MIB),
        cost_estimate=pl.CostEstimate(flops=3 * 10**9, bytes_accessed=6 * MIB, transcendentals=0),
        name="components",
    )(local_idx, kern, in_vmem(eigvecs), *rest)


def pred_kernel(comp_ref, kern16, *rest):
    coef_refs = rest[:8]
    out_ref, acc = rest[8:]
    coefs = jnp.concatenate([ref[...] for ref in coef_refs], axis=0)
    acc[...] = jnp.dot(coefs, kern16[...], preferred_element_type=F32)
    for c in range(N_CTR):
        out_ref[c, 0:16, :] = comp_ref[c * 16:(c + 1) * 16, :]
    bat = lax.axis_index("bat")
    z = bat // 2
    core = bat % 2
    for p, k in enumerate(SHIFTS):
        for s in range(2):
            from_z = (z + N_Z - k) % N_Z
            from_core = core if s == 0 else 1 - core
            first = (2 * p + s) * 32
            for i in range(8):
                out_ref[from_core * 8 + i, pl.ds(16 + from_z * 4, 4), :] = acc[first + 4 * i:first + 4 * i + 4]


def predict(comp, kern16, pieces):
    return pl.pallas_call(
        pred_kernel,
        in_specs=[VMEM] * 10,
        out_specs=VMEM,
        out_shape=jax.ShapeDtypeStruct((N_CTR, 32, LANES), F32),
        scratch_shapes=[pltpu.VMEM((256, LANES), F32)],
        compiler_params=pltpu.CompilerParams(vmem_limit_bytes=16 * MIB),
        name="predict",
    )(comp, kern16, *[in_vmem(x) for x in pieces])


def split2(x):
    hi = x.astype(BF16)
    return hi, (x - hi.astype(F32)).astype(BF16)


def residual_of(ref, targets_ref, core, from_core, z):
    lanes = pl.ds(pl.multiple_of((2 * z + from_core) * LANES, LANES), LANES)
    pred = [ref[(core * 8 + i) * N_Z + z, 16:20, :] for i in range(8)]
    return lanes, jnp.concatenate(pred, axis=0) - targets_ref[:, lanes]


def projected(ref, z, residual):
    comp = jnp.concatenate([ref[c * N_Z + z, 0:16, :] for c in range(N_CTR)], axis=0)
    hi, lo = split2(comp)
    grad = residual.astype(BF16)
    dims = (((1,), (1,)), ((), ()))
    return lax.dot_general(grad, hi, dims, preferred_element_type=F32) + lax.dot_general(
        grad, lo, dims, preferred_element_type=F32
    )


def same_kernel(same_ref, targets_ref, proj_ref):
    core = lax.axis_index("bat") % 2
    proj = jnp.zeros(proj_ref.shape, F32)
    for z in range(N_Z):
        _, residual = residual_of(same_ref, targets_ref, core, core, z)
        proj += projected(same_ref, z, residual)
    proj_ref[...] = proj


def same_part(same, targets, q):
    return pl.pallas_call(
        same_kernel,
        in_specs=[VMEM, VMEM],
        out_specs=VMEM,
        out_shape=jax.ShapeDtypeStruct((targets.shape[0], q), F32),
        compiler_params=pltpu.CompilerParams(vmem_limit_bytes=16 * MIB),
        name="same_part",
    )(same, targets)


def final_kernel(same_ref, other_ref, proj_ref, targets_ref, corr_ref, eig_ref, res_ref, upd_ref):
    core = lax.axis_index("bat") % 2
    proj = proj_ref[...]
    for z in range(N_Z):
        lanes, residual = residual_of(same_ref, targets_ref, core, core, z)
        res_ref[:, lanes] = residual
        lanes, residual = residual_of(other_ref, targets_ref, core, 1 - core, z)
        res_ref[:, lanes] = residual
        proj += projected(other_ref, z, residual)
    scaled = jnp.concatenate(split2(proj * corr_ref[...]), axis=0)
    upd = lax.dot_general(
        scaled, eig_ref[...], (((1,), (1,)), ((), ())), preferred_element_type=F32
    )
    upd_ref[...] = upd[0:32] + upd[32:64]


def final(same, other, proj, targets, correction, eigvecs):
    cols, n = targets.shape
    m_rows, q = eigvecs.shape
    return pl.pallas_call(
        final_kernel,
        in_specs=[VMEM] * 6,
        out_specs=[VMEM, VMEM],
        out_shape=[
            jax.ShapeDtypeStruct((cols, n), F32),
            jax.ShapeDtypeStruct((cols, m_rows), F32),
        ],
        compiler_params=pltpu.CompilerParams(vmem_limit_bytes=16 * MIB),
        name="final",
    )(same, other, proj, targets, correction, in_vmem(eigvecs))


def per_device(table, coefs, targets, eigvecs, correction, batch_idx, nystrom_idx):
    c_rows = table.shape[0]
    idx_row = batch_idx.reshape(1, -1)
    picked = pick(batch_idx, table)
    picked, idx_row, own = lax.optimization_barrier((picked, idx_row, coefs.T))
    from_z = [lax.ppermute(own, "bat", z_shift(k)) if k else own for k in SHIFTS]
    received = lax.all_to_all(picked, "ctr", 0, 0).reshape(-1, D)
    rounds = count_rounds(idx_row, c_rows)
    received, rounds = lax.optimization_barrier((received, rounds))

    def further(state):
        at_round, more = state
        sent = pick(batch_idx, table, at_round.reshape(1))
        got = lax.all_to_all(sent, "ctr", 0, 0).reshape(-1, D)
        return at_round + 1, settle(at_round.reshape(1), idx_row, got, more, c_rows)

    none = jnp.zeros((batch_idx.shape[0], D), BF16)
    _, more = lax.while_loop(lambda state: state[0] < rounds[0], further, (jnp.int32(1), none))
    kern, kern16, local_idx = kernel_rows(
        idx_row, received, more, nystrom_idx.reshape(-1, LANES), table
    )
    local_idx = local_idx.reshape(-1)
    comp, = components(0, local_idx, kern, eigvecs)
    comp, late, *arrived = lax.optimization_barrier((comp, *from_z))
    own_swapped, *swapped = [lax.ppermute(x, "bat", SWAP) for x in (late, *arrived)]
    comp, *arrived = components(1, local_idx, kern, eigvecs, comp, *arrived)
    pieces = [x for pair in zip((own, *arrived), (own_swapped, *swapped)) for x in pair]
    partial = predict(comp, kern16, pieces)
    mine = jnp.sum(lax.all_to_all(partial, "ctr", 0, 0), axis=0)
    comp = jnp.broadcast_to(mine[None, :16], (N_Z, 16, LANES))
    pred = jnp.pad(mine[16:].reshape(N_Z, 4, LANES), ((0, 0), (0, 4), (0, 0)))
    sent = jnp.concatenate([comp, pred], axis=1)
    sent = jnp.broadcast_to(sent[None], (N_CTR,) + sent.shape).reshape((-1,) + sent.shape[1:])
    same = lax.all_to_all(sent, ("ctr", "bat"), 0, 0, axis_index_groups=SAME_CORE)
    other = lax.ppermute(same, "bat", SWAP)
    proj = same_part(same, targets.T, eigvecs.shape[1])
    residual, update = final(same, other, proj, targets.T, correction[None], eigvecs)
    return residual.T, update.T


def solution(mesh):
    return jax.shard_map(
        per_device,
        mesh=mesh,
        in_specs=(
            P("ctr", None),
            P("ctr", "bat"),
            P(None, "bat"),
            P("ctr", None),
            P(),
            P("bat"),
            P("ctr"),
        ),
        out_specs=(P(None, "bat"), P("ctr", "bat")),
        check_vma=False,
    )
```

```python
import functools

import jax
import jax.numpy as jnp
from jax import lax
from jax.experimental import pallas as pl
from jax.experimental.pallas import tpu as pltpu
from jax.sharding import PartitionSpec as P

D = 1024
SHARPNESS = 4.0 / D
N_CTR = 16
N_Z = 4
SHIFTS = (0, 1, 3, 2)
LANES = 128
GROUP = 16
SLOTS = 24
PARTS = ((0, 2048), (2048, 2048))
MIB = 2**20
F32 = jnp.float32
BF16 = jnp.bfloat16
SMEM = pl.BlockSpec(memory_space=pltpu.SMEM)
VMEM = pl.BlockSpec(memory_space=pltpu.VMEM)
HBM = pl.BlockSpec(memory_space=pltpu.HBM)
ANY = pl.BlockSpec(memory_space=pl.ANY)
SWAP = [(i, i ^ 1) for i in range(2 * N_Z)]
SAME_CORE = [[c * 8 + z * 2 + k for c in range(N_CTR) for z in range(N_Z)] for k in range(2)]


def z_shift(k):
    return [(z * 2 + c, (z + k) % N_Z * 2 + c) for z in range(N_Z) for c in range(2)]


def in_vmem(x):
    return pltpu.with_memory_space_constraint(x, pltpu.VMEM)


def in_hbm(x):
    return pltpu.with_memory_space_constraint(x, pltpu.HBM)


def pick_kernel(first, *refs):
    done = 0 if first else refs[0][0] * SLOTS
    idx_hbm, table_ref, out_ref, idx_ref, listed, groups, rows, sems = refs[0 if first else 1:]
    n = idx_ref.shape[0]
    c_rows = table_ref.shape[0]
    first_row = lax.axis_index("ctr") * c_rows
    idx_copy = pltpu.make_async_copy(idx_hbm, idx_ref, sems.at[SLOTS])
    idx_copy.start()
    rows[...] = jnp.zeros_like(rows)
    idx_copy.wait()

    def note(i, count):
        pos = idx_ref[i] - first_row
        listed[count] = pos
        return count + jnp.where((pos >= 0) & (pos < c_rows), 1, 0)

    count = jnp.clip(lax.fori_loop(0, n, note, 0, unroll=32) - done, 0, SLOTS)

    def copy_of(s):
        start = pl.multiple_of(listed[done + s] // GROUP * GROUP, GROUP)
        return pltpu.make_async_copy(table_ref.at[pl.ds(start, GROUP)], groups.at[s], sems.at[s])

    def start(s, carry):
        copy_of(s).start()
        return carry

    def finish(s, carry):
        copy_of(s).wait()
        group = groups[s].astype(F32)
        place = lax.broadcasted_iota(jnp.int32, group.shape, 0)
        kept = jnp.where(place == listed[done + s] % GROUP, group, 0.0)
        rows[pl.ds(s, 1), :] = jnp.sum(kept, axis=0, keepdims=True)
        return carry

    lax.fori_loop(0, count, start, 0)
    lax.fori_loop(0, count, finish, 0)
    packed = rows[...].astype(BF16)
    for c in range(N_CTR):
        out_ref[c] = packed


def pick(batch_idx, table, at_round=None):
    n = batch_idx.shape[0]
    first = at_round is None
    return pl.pallas_call(
        functools.partial(pick_kernel, first),
        in_specs=([] if first else [SMEM]) + [HBM, HBM],
        out_specs=VMEM,
        out_shape=jax.ShapeDtypeStruct((N_CTR, SLOTS, D), BF16),
        scratch_shapes=[
            pltpu.SMEM((n,), jnp.int32),
            pltpu.SMEM((n + 1,), jnp.int32),
            pltpu.VMEM((SLOTS, GROUP, D), BF16),
            pltpu.VMEM((SLOTS, D), F32),
            pltpu.SemaphoreType.DMA((SLOTS + 1,)),
        ],
        compiler_params=pltpu.CompilerParams(vmem_limit_bytes=8 * MIB),
        name="pick",
    )(*([] if first else [at_round]), in_hbm(batch_idx), in_hbm(table))


def owners(idx_row, c_rows):
    n = idx_row.shape[1]
    row = (idx_row // c_rows).astype(F32)
    i = lax.broadcasted_iota(jnp.int32, (n, n), 0)
    j = lax.broadcasted_iota(jnp.int32, (n, n), 1)
    column = jnp.sum(jnp.where(i == j, row, 0.0), axis=1, keepdims=True)
    return column, column == row, j < i


def count_kernel(c_rows, idx_ref, rounds_ref):
    _, alike, _ = owners(idx_ref[...], c_rows)
    most = jnp.max(jnp.sum(jnp.where(alike, 1.0, 0.0), axis=1, keepdims=True))
    rounds_ref[0] = (most.astype(jnp.int32) + SLOTS - 1) // SLOTS


def count_rounds(idx_row, c_rows):
    return pl.pallas_call(
        functools.partial(count_kernel, c_rows),
        in_specs=[VMEM],
        out_specs=SMEM,
        out_shape=jax.ShapeDtypeStruct((1,), jnp.int32),
        cost_estimate=pl.CostEstimate(flops=10**9, bytes_accessed=MIB, transcendentals=0),
        name="count_rounds",
    )(idx_row)


def settled(idx_row, received, at_round, c_rows):
    n = idx_row.shape[1]
    owner, alike, earlier = owners(idx_row, c_rows)
    before = alike & earlier
    slot = jnp.sum(jnp.where(before, 1.0, 0.0), axis=1, keepdims=True) - at_round * SLOTS
    here = (slot >= 0.0) & (slot < SLOTS)
    place = jnp.where(here, owner * SLOTS + slot, -1.0)
    column = lax.broadcasted_iota(jnp.int32, (n, N_CTR * SLOTS), 1).astype(F32)
    chosen = jnp.where(column == place, 1.0, 0.0).astype(BF16)
    return jnp.dot(chosen, received, preferred_element_type=F32)


def settle_kernel(c_rows, round_ref, idx_ref, received_ref, before_hbm, out_hbm, rows_ref, sem):
    copy_in = pltpu.make_async_copy(before_hbm, rows_ref, sem)
    copy_in.start()
    rows = settled(idx_ref[...], received_ref[...], round_ref[0].astype(F32), c_rows)
    copy_in.wait()
    rows_ref[...] = (rows + rows_ref[...].astype(F32)).astype(BF16)
    copy_out = pltpu.make_async_copy(rows_ref, out_hbm, sem)
    copy_out.start()
    copy_out.wait()


def settle(at_round, idx_row, received, before, c_rows):
    return pl.pallas_call(
        functools.partial(settle_kernel, c_rows),
        in_specs=[SMEM, VMEM, VMEM, HBM],
        out_specs=HBM,
        out_shape=jax.ShapeDtypeStruct(before.shape, BF16),
        scratch_shapes=[pltpu.VMEM(before.shape, BF16), pltpu.SemaphoreType.DMA(())],
        compiler_params=pltpu.CompilerParams(vmem_limit_bytes=8 * MIB),
        name="settle",
    )(at_round, idx_row, received, in_hbm(before))


N_TILES = 8


def kern_kernel(
    idx_ref, received_in, more_in, nys_ref, table_ref, kern, kern16, local_ref,
    held, received_ref, more_ref, pts_ref, cross, sems
):
    n_tiles = sems.shape[0] - 2
    c_rows = held.shape[0]
    tile = c_rows // n_tiles

    def rows_of(i):
        return pl.ds(pl.multiple_of(i * tile, tile), tile)

    def copy_of(i):
        rows = rows_of(i)
        return pltpu.make_async_copy(table_ref.at[rows], held.at[rows], sems.at[i])

    received_copy = pltpu.make_async_copy(received_in, received_ref, sems.at[n_tiles])
    more_copy = pltpu.make_async_copy(more_in, more_ref, sems.at[n_tiles + 1])
    received_copy.start()
    more_copy.start()
    for i in range(n_tiles):
        copy_of(i).start()
    local_ref[...] = nys_ref[...] - lax.axis_index("ctr") * c_rows
    received_copy.wait()
    more_copy.wait()
    pts = settled(idx_ref[...], received_ref[...], 0.0, c_rows) + more_ref[...].astype(F32)
    pts_ref[...] = pts.astype(BF16)
    n = pts.shape[0]
    on_diagonal = lax.broadcasted_iota(jnp.int32, (n, n), 0) == lax.broadcasted_iota(jnp.int32, (n, n), 1)
    sums = jnp.sum(pts * pts, axis=1, keepdims=True)
    pts_sq = jnp.sum(jnp.where(on_diagonal, sums, 0.0), axis=0, keepdims=True)

    def multiply(i):
        copy_of(i).wait()
        cross[i % 2] = lax.dot_general(
            held[rows_of(i), :], pts_ref[...], (((1,), (1,)), ((), ())),
            preferred_element_type=F32,
        )

    def finish(i):
        wide = held[rows_of(i), :].astype(F32)
        row_sq = jnp.sum(wide * wide, axis=1, keepdims=True)
        k = jnp.exp(-SHARPNESS * (row_sq + pts_sq - 2.0 * cross[i % 2])).astype(BF16)
        kern[rows_of(i), :] = k.astype(F32)
        kern16[rows_of(i), :] = k

    def both(i, carry):
        multiply(i)
        finish(i - 1)
        return carry

    multiply(0)
    lax.fori_loop(1, n_tiles, both, 0)
    finish(n_tiles - 1)


def kernel_rows(idx_row, received, more, nystrom_idx, table):
    c_rows = table.shape[0]
    n = idx_row.shape[1]
    return pl.pallas_call(
        kern_kernel,
        in_specs=[VMEM, ANY, ANY, VMEM, HBM],
        out_specs=[VMEM, VMEM, VMEM],
        out_shape=[
            jax.ShapeDtypeStruct((c_rows, n), F32),
            jax.ShapeDtypeStruct((c_rows, n), BF16),
            jax.ShapeDtypeStruct(nystrom_idx.shape, jnp.int32),
        ],
        scratch_shapes=[
            pltpu.VMEM((c_rows, D), BF16),
            pltpu.VMEM(received.shape, BF16),
            pltpu.VMEM((n, D), BF16),
            pltpu.VMEM((n, D), BF16),
            pltpu.VMEM((2, c_rows // N_TILES, n), F32),
            pltpu.SemaphoreType.DMA((N_TILES + 2,)),
        ],
        compiler_params=pltpu.CompilerParams(vmem_limit_bytes=30 * MIB),
        cost_estimate=pl.CostEstimate(flops=10**10, bytes_accessed=24 * MIB, transcendentals=10**6),
        name="kernel_rows",
    )(
        idx_row, received, more, nystrom_idx, in_hbm(table)
    )


def comp_kernel(part, idx_ref, kern, eig_ref, *rest):
    if part:
        n_arrived = rest[-1].shape[0]
        before_ref, *arrived = rest[:1 + n_arrived]
        out_ref, *landed = rest[1 + n_arrived:-2]
        nys, sems = rest[-2:]
        copies = [pltpu.make_async_copy(x, y, sems.at[i]) for i, (x, y) in enumerate(zip(arrived, landed))]
        for copy in copies:
            copy.start()
    else:
        out_ref, nys = rest
    unroll = 128
    first, n = PARTS[part]

    def gather(j, carry):
        for u in range(unroll):
            m = j * unroll + u
            nys[pl.ds(m, 1), :] = kern[pl.ds(idx_ref[first + m], 1), :]
        return carry

    lax.fori_loop(0, n // unroll, gather, 0)
    comp = lax.dot_general(
        eig_ref[first:first + n, :], nys[...].astype(BF16), (((0,), (0,)), ((), ())),
        preferred_element_type=F32,
    )
    if part:
        comp += before_ref[...]
        for copy in copies:
            copy.wait()
    out_ref[...] = comp


def components(part, local_idx, kern, eigvecs, *rest):
    q = eigvecs.shape[1]
    n = kern.shape[1]
    arrived = rest[1:]
    return pl.pallas_call(
        functools.partial(comp_kernel, part),
        in_specs=[SMEM, VMEM, VMEM] + ([VMEM] + [ANY] * len(arrived) if part else []),
        out_specs=[VMEM] * (1 + len(arrived)),
        out_shape=[jax.ShapeDtypeStruct((q, n), F32)]
        + [jax.ShapeDtypeStruct(x.shape, x.dtype) for x in arrived],
        scratch_shapes=[pltpu.VMEM((PARTS[part][1], n), F32)]
        + ([pltpu.SemaphoreType.DMA((len(arrived),))] if part else []),
        compiler_params=pltpu.CompilerParams(vmem_limit_bytes=16 * MIB),
        cost_estimate=pl.CostEstimate(flops=3 * 10**9, bytes_accessed=6 * MIB, transcendentals=0),
        name="components",
    )(local_idx, kern, in_vmem(eigvecs), *rest)


def pred_kernel(comp_ref, kern16, *rest):
    coef_refs = rest[:8]
    out_ref, acc = rest[8:]
    coefs = jnp.concatenate([ref[...] for ref in coef_refs], axis=0)
    acc[...] = jnp.dot(coefs, kern16[...], preferred_element_type=F32)
    for c in range(N_CTR):
        out_ref[c, 0:16, :] = comp_ref[c * 16:(c + 1) * 16, :]
    bat = lax.axis_index("bat")
    z = bat // 2
    core = bat % 2
    for p, k in enumerate(SHIFTS):
        for s in range(2):
            from_z = (z + N_Z - k) % N_Z
            from_core = core if s == 0 else 1 - core
            first = (2 * p + s) * 32
            for i in range(8):
                out_ref[from_core * 8 + i, pl.ds(16 + from_z * 4, 4), :] = acc[first + 4 * i:first + 4 * i + 4]


def predict(comp, kern16, pieces):
    return pl.pallas_call(
        pred_kernel,
        in_specs=[VMEM] * 10,
        out_specs=VMEM,
        out_shape=jax.ShapeDtypeStruct((N_CTR, 32, LANES), F32),
        scratch_shapes=[pltpu.VMEM((256, LANES), F32)],
        compiler_params=pltpu.CompilerParams(vmem_limit_bytes=16 * MIB),
        name="predict",
    )(comp, kern16, *[in_vmem(x) for x in pieces])


def split2(x):
    hi = x.astype(BF16)
    return hi, (x - hi.astype(F32)).astype(BF16)


def residual_of(ref, targets_ref, core, from_core, z):
    lanes = pl.ds(pl.multiple_of((2 * z + from_core) * LANES, LANES), LANES)
    pred = [ref[(core * 8 + i) * N_Z + z, 16:20, :] for i in range(8)]
    return lanes, jnp.concatenate(pred, axis=0) - targets_ref[:, lanes]


def projected(ref, z, residual):
    comp = jnp.concatenate([ref[c * N_Z + z, 0:16, :] for c in range(N_CTR)], axis=0)
    hi, lo = split2(comp)
    grad = residual.astype(BF16)
    dims = (((1,), (1,)), ((), ()))
    return lax.dot_general(grad, hi, dims, preferred_element_type=F32) + lax.dot_general(
        grad, lo, dims, preferred_element_type=F32
    )


def same_kernel(same_ref, targets_ref, proj_ref):
    core = lax.axis_index("bat") % 2
    proj = jnp.zeros(proj_ref.shape, F32)
    for z in range(N_Z):
        _, residual = residual_of(same_ref, targets_ref, core, core, z)
        proj += projected(same_ref, z, residual)
    proj_ref[...] = proj


def same_part(same, targets, q):
    return pl.pallas_call(
        same_kernel,
        in_specs=[VMEM, VMEM],
        out_specs=VMEM,
        out_shape=jax.ShapeDtypeStruct((targets.shape[0], q), F32),
        compiler_params=pltpu.CompilerParams(vmem_limit_bytes=16 * MIB),
        name="same_part",
    )(same, targets)


def final_kernel(same_ref, other_ref, proj_ref, targets_ref, corr_ref, eig_ref, res_ref, upd_ref):
    core = lax.axis_index("bat") % 2
    proj = proj_ref[...]
    for z in range(N_Z):
        lanes, residual = residual_of(same_ref, targets_ref, core, core, z)
        res_ref[:, lanes] = residual
        lanes, residual = residual_of(other_ref, targets_ref, core, 1 - core, z)
        res_ref[:, lanes] = residual
        proj += projected(other_ref, z, residual)
    scaled = jnp.concatenate(split2(proj * corr_ref[...]), axis=0)
    upd = lax.dot_general(
        scaled, eig_ref[...], (((1,), (1,)), ((), ())), preferred_element_type=F32
    )
    upd_ref[...] = upd[0:32] + upd[32:64]


def final(same, other, proj, targets, correction, eigvecs):
    cols, n = targets.shape
    m_rows, q = eigvecs.shape
    return pl.pallas_call(
        final_kernel,
        in_specs=[VMEM] * 6,
        out_specs=[VMEM, VMEM],
        out_shape=[
            jax.ShapeDtypeStruct((cols, n), F32),
            jax.ShapeDtypeStruct((cols, m_rows), F32),
        ],
        compiler_params=pltpu.CompilerParams(vmem_limit_bytes=16 * MIB),
        name="final",
    )(same, other, proj, targets, correction, in_vmem(eigvecs))


def per_device(table, coefs, targets, eigvecs, correction, batch_idx, nystrom_idx):
    c_rows = table.shape[0]
    idx_row = batch_idx.reshape(1, -1)
    picked = pick(batch_idx, table)
    picked, idx_row, own = lax.optimization_barrier((picked, idx_row, coefs.T))
    from_z = [lax.ppermute(own, "bat", z_shift(k)) if k else own for k in SHIFTS]
    received = lax.all_to_all(picked, "ctr", 0, 0).reshape(-1, D)
    rounds = count_rounds(idx_row, c_rows)
    received, rounds = lax.optimization_barrier((received, rounds))

    def further(state):
        at_round, more = state
        sent = pick(batch_idx, table, at_round.reshape(1))
        got = lax.all_to_all(sent, "ctr", 0, 0).reshape(-1, D)
        return at_round + 1, settle(at_round.reshape(1), idx_row, got, more, c_rows)

    none = jnp.zeros((batch_idx.shape[0], D), BF16)
    _, more = lax.while_loop(lambda state: state[0] < rounds[0], further, (jnp.int32(1), none))
    kern, kern16, local_idx = kernel_rows(
        idx_row, received, more, nystrom_idx.reshape(-1, LANES), table
    )
    local_idx = local_idx.reshape(-1)
    comp, = components(0, local_idx, kern, eigvecs)
    comp, late, *arrived = lax.optimization_barrier((comp, *from_z))
    own_swapped, *swapped = [lax.ppermute(x, "bat", SWAP) for x in (late, *arrived)]
    comp, *arrived = components(1, local_idx, kern, eigvecs, comp, *arrived)
    pieces = [x for pair in zip((own, *arrived), (own_swapped, *swapped)) for x in pair]
    partial = predict(comp, kern16, pieces)
    mine = jnp.sum(lax.all_to_all(partial, "ctr", 0, 0), axis=0)
    comp = jnp.broadcast_to(mine[None, :16], (N_Z, 16, LANES))
    pred = jnp.pad(mine[16:].reshape(N_Z, 4, LANES), ((0, 0), (0, 4), (0, 0)))
    sent = jnp.concatenate([comp, pred], axis=1)
    sent = jnp.broadcast_to(sent[None], (N_CTR,) + sent.shape).reshape((-1,) + sent.shape[1:])
    same = lax.all_to_all(sent, ("ctr", "bat"), 0, 0, axis_index_groups=SAME_CORE)
    other = lax.ppermute(same, "bat", SWAP)
    proj = same_part(same, targets.T, eigvecs.shape[1])
    residual, update = final(same, other, proj, targets.T, correction[None], eigvecs)
    return residual.T, update.T


def solution(mesh):
    return jax.shard_map(
        per_device,
        mesh=mesh,
        in_specs=(
            P("ctr", None),
            P("ctr", "bat"),
            P(None, "bat"),
            P("ctr", None),
            P(),
            P("bat"),
            P("ctr"),
        ),
        out_specs=(P(None, "bat"), P("ctr", "bat")),
        check_vma=False,
    )
```
